32 devices in a mesh: walker: 4 (over x, core), prow: 2 (over y), pcol: 4 (over z).
Axes of the slice: x: 2, y: 2, z: 4, core: 2. Of those that a mesh axis runs over, the one named last changes fastest.
Arguments:
- o_rows: bfloat16 [8192, 2048], P('walker', ('prow', 'pcol')), may hold values from -21 to 21
- o_cols: bfloat16 [8192, 4096], P('walker', ('pcol', 'prow')), may hold values from -48 to 48
- grad_energy: bfloat16 [8192, 4096], P('walker', ('pcol', 'prow')), may hold values from -8 to 8
- energy: float32 [8192], P('walker'), may hold values from -5 to 1
Outputs:
- hamil: float32 [2048, 4096], P(('prow', 'walker'), 'pcol')
- correlation: float32 [2048, 4096], P(('prow', 'walker'), 'pcol')
The draws below stay inside these ranges and needn't reach their ends.
All inputs are finite; a program needn't handle non-finite values.
Results may differ from the reference program's by a relative error of at most 0.008.
Values may be sent and summed in bfloat16 or wider, within the bound.
No kernel may reach another device: no remote copies, remote signals or barrier semaphores. Data moves between devices by JAX's collectives and lax.ppermute only.
A program may use at most 128 MiB of HBM per device.

```python
import jax
import jax.numpy as jnp
from jax import lax

SAMPLES = 8192
ROWS = 2048
NCOL = 4096


def noise_field(key, shape):
    return jnp.clip(jax.random.normal(key, shape, jnp.float32), -4.0, 4.0)


def sample_scale():
    return 0.5 + jnp.arange(SAMPLES, dtype=jnp.float32) / SAMPLES


def offsets(key, count):
    return jax.random.uniform(key, (count,), jnp.float32, -2.0, 2.0)


def col_scales(key, count):
    return jnp.exp(jax.random.uniform(key, (count,), jnp.float32, jnp.log(0.3), jnp.log(3.0)))


def shared_base(key):
    return noise_field(jax.random.fold_in(key, 1), (SAMPLES, ROWS))


def tiled_base(key):
    return jnp.tile(shared_base(key), (1, NCOL // ROWS))


def draw_o_rows(key, part):
    base = shared_base(key)
    shift = offsets(jax.random.fold_in(key, 2), ROWS)
    spread = col_scales(jax.random.fold_in(key, 3), ROWS)
    values = sample_scale()[:, None] * (shift + spread * base)
    return values.astype(jnp.bfloat16)


def draw_o_cols(key, part):
    tiled = tiled_base(key)
    mixing = jax.random.uniform(jax.random.fold_in(key, 4), (NCOL,), jnp.float32, 0.5, 1.5)
    own_part = noise_field(jax.random.fold_in(key, 5), (SAMPLES, NCOL))
    spread = col_scales(jax.random.fold_in(key, 6), NCOL)
    shift = offsets(jax.random.fold_in(key, 7), NCOL)
    values = sample_scale()[:, None] * (shift + spread * (mixing * tiled + own_part))
    return values.astype(jnp.bfloat16)


def draw_grad_energy(key, part):
    tiled = tiled_base(key)
    factor = jax.random.uniform(jax.random.fold_in(key, 8), (NCOL,), jnp.float32, 0.5, 1.5)
    extra = noise_field(jax.random.fold_in(key, 9), (SAMPLES, NCOL))
    return (factor * tiled + 0.5 * extra).astype(jnp.bfloat16)


def draw_energy(key, part):
    extra = noise_field(jax.random.fold_in(key, 10), (SAMPLES,))
    return -(0.5 + 1.5 * sample_scale()) + 0.5 * extra


def setup_inputs(seed: int = 0) -> dict:
    key_list = jax.random.split(jax.random.key(seed), 5)
    o_rows = draw_o_rows(jax.random.fold_in(key_list[4], 71), 0)
    o_cols = draw_o_cols(jax.random.fold_in(key_list[4], 71), 0)
    grad_energy = draw_grad_energy(jax.random.fold_in(key_list[4], 71), 0)
    energy = draw_energy(jax.random.fold_in(key_list[4], 71), 0)
    return dict(o_rows=o_rows, o_cols=o_cols, grad_energy=grad_energy, energy=energy)


def reference(o_rows, o_cols, grad_energy, energy):
    row_mean = jnp.sum(o_rows.astype(jnp.float32), axis=0) / SAMPLES
    col_mean = jnp.sum(o_cols.astype(jnp.float32), axis=0) / SAMPLES
    d_rows = (o_rows.astype(jnp.float32) - row_mean).astype(jnp.bfloat16)
    d_cols = (o_cols.astype(jnp.float32) - col_mean).astype(jnp.bfloat16)
    weighted = (energy[:, None] * d_cols.astype(jnp.float32) + grad_energy.astype(jnp.float32)).astype(jnp.bfloat16)
    dims = (((0,), (0,)), ((), ()))
    correlation = lax.dot_general(d_rows, d_cols, dims, preferred_element_type=jnp.float32) / SAMPLES
    hamil = lax.dot_general(d_rows, weighted, dims, preferred_element_type=jnp.float32) / SAMPLES
    return hamil, correlation
```

```python
import functools

import jax
import jax.numpy as jnp
from jax import lax
from jax.experimental import pallas as pl
from jax.experimental.pallas import tpu as pltpu
from jax.sharding import PartitionSpec as P

BF = jnp.bfloat16
F32 = jnp.float32
VMEM = pl.BlockSpec(memory_space=pltpu.VMEM)
SMEM = pl.BlockSpec(memory_space=pltpu.SMEM)
MID, LOW, CORE, STRAIGHT, TABLE = 0, 1, 2, 3, 4


def call(kernel, outs, *args, scratch=(), limit=40):
    return pl.pallas_call(
        kernel,
        out_shape=[jax.ShapeDtypeStruct(s, d) for s, d in outs],
        in_specs=[SMEM if a.dtype == jnp.int32 else VMEM for a in args],
        out_specs=[VMEM] * len(outs),
        scratch_shapes=list(scratch),
        compiler_params=pltpu.CompilerParams(vmem_limit_bytes=limit * 2**20),
        cost_estimate=pl.CostEstimate(flops=0, bytes_accessed=0, transcendentals=0),
    )(*args)


def after(value, *others):
    return lax.optimization_barrier((value,) + others)[0]


def centred(values, mean):
    return (values.astype(F32) - mean).astype(BF)


def weigh(energy, cols, grads):
    return (energy * cols.astype(F32) + grads.astype(F32)).astype(BF)


def dot(rows, right):
    return lax.dot_general(rows, right, (((0,), (0,)), ((), ())), preferred_element_type=F32)


def sums_kernel(rows, cols, out):
    width = rows.shape[1]
    out[:, :width] = jnp.sum(rows[...].astype(F32), axis=0, keepdims=True)
    out[:, width:] = jnp.sum(cols[...].astype(F32), axis=0, keepdims=True)


def own_kernel(count, cuts, cols, grads, energy, sums, out, *pieces):
    width = cols.shape[1]
    d = centred(cols[...], sums[:, -width:] / count)
    out[:, :width] = d
    out[:, width:] = weigh(energy[...], d, grads[...])
    for a, b, piece in zip(cuts[:-1], cuts[1:], pieces):
        piece[...] = grads[:, a:b]


def store_pieces(result, blocks, piece, core, send, keep, at, cols):
    for i in range(blocks[1]):
        walker = blocks[0] * blocks[1] + i
        value = result[i * piece : (i + 1) * piece].astype(BF)
        slot = at[walker]

        @pl.when(core == walker % 2)
        def _():
            keep[slot, :, cols] = value

        @pl.when(core != walker % 2)
        def _():
            send[slot, :, cols] = value


def group_products(info, tile, rights, blocks, per, slots, send, keep):
    piece = tile.shape[2] // per
    for j, b in enumerate(blocks):
        start = 0
        for right in rights:
            n = right.shape[1]
            store_pieces(
                dot(tile[j], right[...]),
                (b, per),
                piece,
                info[CORE],
                send,
                keep,
                slots,
                slice(start, start + n),
            )
            start += n


def early_kernel(
    count, per, slots,
    info, own_rows, near, mid1, mid2, m0, m1, m2, m3, ow, far_raw, far_sums,
    send, keep, tile, far,
):
    rw, cw = own_rows.shape[1], far_raw.shape[1]
    mid, low = info[MID] == 1, info[LOW] == 1
    far[...] = centred(far_raw[...], far_sums[:, rw:] / count)
    there = info[LOW]

    @pl.when(mid)
    def _():
        tile[there] = centred(mid1[...], m3[:, :rw] / count)
        tile[1 - there] = centred(own_rows[...], m0[:, :rw] / count)

    @pl.when(jnp.logical_not(mid))
    def _():
        tile[there] = centred(mid2[...], m2[:, :rw] / count)
        tile[1 - there] = centred(near[...], m1[:, :rw] / count)

    half = ow.shape[1] // 2
    group_products(
        info, tile, (ow.at[:, :half], ow.at[:, half:], far), (1, 2), per, slots, send, keep
    )


def late_kernel(
    count, per, slots,
    info, own_rows, near, last1, last2, m0, m1, m2, m3, ow, far,
    send, keep, tile,
):
    rw = own_rows.shape[1]
    mid = info[MID] == 1
    there = info[LOW]

    @pl.when(mid)
    def _():
        tile[there] = centred(last1[...], m2[:, :rw] / count)
        tile[1 - there] = centred(near[...], m1[:, :rw] / count)

    @pl.when(jnp.logical_not(mid))
    def _():
        tile[there] = centred(last2[...], m3[:, :rw] / count)
        tile[1 - there] = centred(own_rows[...], m0[:, :rw] / count)

    half = ow.shape[1] // 2
    group_products(
        info, tile, (ow.at[:, :half], ow.at[:, half:], far), (0, 3), per, slots, send, keep
    )


def chunk_kernel(start, per, slots, info, early, late, far, energy, grads, send, keep, right):
    n = grads.shape[1]
    right[...] = weigh(energy[...], far[:, start : start + n], grads[...])
    group_products(info, early, (right,), (1, 2), per, slots, send, keep)
    group_products(info, late, (right,), (0, 3), per, slots, send, keep)


def pair_kernel(first, pieces, info, keep, got, *outs):
    for k, out in enumerate(outs, 1):
        i = jnp.clip(info[TABLE + k] - first, 0, pieces - 1)
        out[...] = (keep[i].astype(F32) + got[i].astype(F32)).astype(BF)


def final_kernel(count, shapes, info, *refs):
    ham, corr = refs[-2:]
    cw = ham.shape[1] // 2
    straight = info[STRAIGHT] == 1
    pos = info[TABLE]

    def put(out, near, start, value):
        value = value / count

        @pl.when(straight == near)
        def _():
            out[:, start : start + value.shape[1]] = value

        @pl.when(straight != near)
        def _():
            out[:, cw + start : cw + start + value.shape[1]] = value

    at = 0
    for shifts, first, pieces, parts in shapes:
        keep, got = refs[at], refs[at + 1]
        others = refs[at + 2 : at + 2 + shifts]
        at += 2 + shifts

        @pl.when((pos >= first) & (pos < first + pieces))
        def _():
            i = pos - first
            for name, near, a, b, start in parts:
                value = keep[i, :, a:b].astype(F32) + got[i, :, a:b].astype(F32)
                for other in others:
                    value = value + other[:, a:b].astype(F32)
                put(ham if name == "ham" else corr, near, start, value)


def per_device(o_rows, o_cols, grad_energy, energy):
    samples, rw = o_rows.shape
    cw = o_cols.shape[1]
    walkers = lax.axis_size("walker")
    chips = walkers // 2
    per = walkers // 4
    piece = rw // per
    w, y, z = (lax.axis_index(a) for a in ("walker", "prow", "pcol"))
    count = samples * walkers
    flip = [(0, 1), (1, 0)]
    outer = [(0, 1), (1, 0), (2, 3), (3, 2)]
    inner = [(1, 2), (2, 1)]
    ends = [(1, 0), (2, 3)]
    other_core = [(v, v ^ 1) for v in range(walkers)]

    order = [b * per + i for b in (1, 2, 0, 3) for i in range(per)]
    place = {v: [u for u in order if u % 2 == v % 2].index(v) for v in order}
    late_slots = {v: place[v] - per for v in order}
    table = [[place[(v + 2 * k) % walkers] for k in range(chips)] for v in range(walkers)]
    info = jnp.concatenate(
        (
            jnp.stack(((z == 1) | (z == 2), z < 2, w % 2, y == 0)).astype(jnp.int32),
            jnp.asarray(table, jnp.int32)[w],
        )
    )

    def shift(k, first, pieces):
        return [
            (v, (v + 2 * k) % walkers)
            for v in range(walkers)
            if first <= table[v][k] < first + pieces
        ]

    far_raw = lax.ppermute(o_cols, "prow", flip)
    near = lax.ppermute(o_rows, "pcol", outer)
    mid1 = lax.ppermute(o_rows, "pcol", inner)

    (sums,) = call(sums_kernel, [((1, rw + cw), F32)], o_rows, o_cols)
    m0 = lax.psum(sums, "walker")
    m1 = lax.ppermute(m0, "pcol", outer)
    m2 = lax.ppermute(m0, "pcol", [(0, 2), (1, 3), (2, 0), (3, 1)])

    column = energy[:, None]
    cuts = [0, cw // 2, 3 * cw // 4, cw]
    widths = [b - a for a, b in zip(cuts[:-1], cuts[1:])]
    ow, *grads = call(
        functools.partial(own_kernel, count, cuts),
        [((samples, 2 * cw), BF)] + [((samples, n), BF) for n in widths],
        o_cols, grad_energy, column, m0,
    )

    near, mid1, m1, m2, ow, m0 = lax.optimization_barrier((near, mid1, m1, m2, ow, m0))
    m3 = lax.ppermute(m0, "pcol", [(0, 3), (1, 2), (2, 1), (3, 0)])
    far_sums = lax.ppermute(m0, "prow", flip)
    mid2 = lax.ppermute(mid1, "pcol", ends)
    last1 = lax.ppermute(near, "pcol", inner)
    far_grads = [lax.ppermute(after(grads[0], m3), "prow", flip)]

    mid2, last1, far_raw, far_sums, m3, grads[1] = lax.optimization_barrier(
        (mid2, last1, far_raw, far_sums, m3, grads[1])
    )
    last2 = lax.ppermute(last1, "pcol", ends)
    far_grads.append(lax.ppermute(grads[1], "prow", flip))

    n1 = 3 * cw
    group = [((per, piece, n1), BF), ((per, piece, n1), BF)]
    tile_shape = ((2, samples, rw), BF)
    e_send, e_keep, early, far = call(
        functools.partial(early_kernel, count, per, place),
        group + [tile_shape, ((samples, cw), BF)],
        info, o_rows, near, mid1, mid2, m0, m1, m2, m3, ow, far_raw, far_sums,
    )

    messages = []

    def reduce(send, keep, first, pieces, parts):
        got = lax.ppermute(send, "walker", other_core)
        sent = call(
            functools.partial(pair_kernel, first, pieces),
            [(keep.shape[1:], BF)] * (chips - 1),
            info, keep, got,
        )
        others = [
            lax.ppermute(s, "walker", shift(k, first, pieces)) for k, s in enumerate(sent, 1)
        ]
        messages.append((keep, got, others, first, pieces, parts))

    parts = [
        ("corr", True, 0, cw, 0),
        ("ham", True, cw, 2 * cw, 0),
        ("corr", False, 2 * cw, 3 * cw, 0),
    ]
    reduce(e_send, e_keep, 0, per, parts)

    last2, far_grads[0], grads[2] = lax.optimization_barrier((last2, far_grads[0], grads[2]))
    far_grads.append(lax.ppermute(grads[2], "prow", flip))
    l_send, l_keep, late = call(
        functools.partial(late_kernel, count, per, late_slots),
        group + [tile_shape],
        info, o_rows, near, last1, last2, m0, m1, m2, m3, ow, far,
    )
    reduce(l_send, l_keep, per, per, parts)

    for a, n, g in zip(cuts, widths, far_grads):
        send, keep = call(
            functools.partial(chunk_kernel, a, per, place),
            [((2 * per, piece, n), BF)] * 2,
            info, early, late, far, column, g,
            scratch=[pltpu.VMEM((samples, n), BF)],
        )
        reduce(send, keep, 0, 2 * per, [("ham", False, 0, n, a)])

    flat, shapes = [], []
    for keep, got, others, first, pieces, parts in messages:
        flat += [keep, got, *others]
        shapes.append((len(others), first, pieces, parts))
    return call(
        functools.partial(final_kernel, count, shapes),
        [((piece, 2 * cw), F32)] * 2,
        info, *flat,
    )


def solution(mesh):
    in_specs = (
        P("walker", ("prow", "pcol")),
        P("walker", ("pcol", "prow")),
        P("walker", ("pcol", "prow")),
        P("walker"),
    )
    out_specs = (P(("prow", "walker"), "pcol"), P(("prow", "walker"), "pcol"))

    def per(*args):
        return tuple(per_device(*args))

    return jax.shard_map(
        per, mesh=mesh, in_specs=in_specs, out_specs=out_specs, check_vma=False
    )
```

```python
import functools

import jax
import jax.numpy as jnp
from jax import lax
from jax.experimental import pallas as pl
from jax.experimental.pallas import tpu as pltpu
from jax.sharding import PartitionSpec as P

BF = jnp.bfloat16
F32 = jnp.float32
VMEM = pl.BlockSpec(memory_space=pltpu.VMEM)
SMEM = pl.BlockSpec(memory_space=pltpu.SMEM)
MID, LOW, CORE, STRAIGHT, TABLE = 0, 1, 2, 3, 4
MEAN_COST, FAR_COST, FIRST_COST, LAST_COST = 6, 3, 0, 4
WEIGH_COSTS, GATHER_COST = (0, 0, 12), 3


def call(kernel, outs, *args, scratch=(), limit=24, cost=0):
    return pl.pallas_call(
        kernel,
        out_shape=[jax.ShapeDtypeStruct(s, d) for s, d in outs],
        in_specs=[SMEM if a.dtype == jnp.int32 else VMEM for a in args],
        out_specs=[VMEM] * len(outs),
        scratch_shapes=list(scratch),
        compiler_params=pltpu.CompilerParams(vmem_limit_bytes=limit * 2**20),
        cost_estimate=pl.CostEstimate(
            flops=int(cost * 1.15e9), bytes_accessed=0, transcendentals=0
        ),
    )(*args)


def after(value, *others):
    return lax.optimization_barrier((value,) + others)[0]


def centred(values, mean):
    return (values.astype(F32) - mean).astype(BF)


def weigh(energy, cols, grads):
    return (energy * cols.astype(F32) + grads.astype(F32)).astype(BF)


def dot(rows, right):
    return lax.dot_general(rows, right, (((0,), (0,)), ((), ())), preferred_element_type=F32)


def sums_kernel(rows, cols, out):
    width = rows.shape[1]
    out[:, :width] = jnp.sum(rows[...].astype(F32), axis=0, keepdims=True)
    out[:, width:] = jnp.sum(cols[...].astype(F32), axis=0, keepdims=True)


def own_kernel(count, cuts, cols, grads, energy, sums, out, wide, *pieces):
    width = cols.shape[1]
    lanes = wide.shape[1]
    d = centred(cols[...], sums[:, -width:] / count)
    out[:, :width] = d
    spread = jnp.broadcast_to(energy[...], wide.shape)
    wide[...] = spread
    for a in range(0, width, lanes):
        b = a + lanes
        out[:, width + a : width + b] = weigh(spread, d[:, a:b], grads[:, a:b])
    for a, b, piece in zip(cuts[:-1], cuts[1:], pieces):
        piece[...] = grads[:, a:b]


def by_core(info, walker, slot, sends, keep, value):
    @pl.when(info[CORE] == walker % 2)
    def _():
        keep[slot] = value

    @pl.when(info[CORE] != walker % 2)
    def _():
        start = 0
        for send in sends:
            width = send.shape[-1]
            send[slot] = value[:, start : start + width]
            start += width


def products(tile, rights):
    return jnp.concatenate([dot(tile, right[...]).astype(BF) for right in rights], axis=1)


def by_block(info, block, axis, per, slots, sends, keep, value):
    piece = value.shape[axis] // per
    for i in range(per):
        at = slice(i * piece, (i + 1) * piece)
        walker = block * per + i
        part = value[at] if axis == 0 else value[:, at]
        by_core(info, walker, slots[walker], sends, keep, part)


def low_or_high(info, then):
    for low in (1, 0):
        pl.when(info[LOW] == low)(functools.partial(then, 0 if low else 3, 3 if low else 0))


def mean_kernel(count, sums, out):
    out[...] = sums[:, -out.shape[1] :] / count


def far_kernel(raw, mean, out):
    out[...] = centred(raw[...], mean[...])


def early_kernel(
    count, per, slots,
    info, own_rows, near, mid1, mid2, m0, m1, m2, m3, ow, far,
    keep, early, *sends,
):
    rw = own_rows.shape[1]

    def group(there, beside):
        @pl.when(info[LOW] == 1)
        def _():
            early[:, rw:] = there
            early[:, :rw] = beside

        @pl.when(info[LOW] == 0)
        def _():
            early[:, :rw] = there
            early[:, rw:] = beside

    @pl.when(info[MID] == 1)
    def _():
        own = centred(own_rows[...], m0[:, :rw] / count)
        group(centred(mid1[...], m3[:, :rw] / count), own)

    @pl.when(info[MID] == 0)
    def _():
        next_to = centred(near[...], m1[:, :rw] / count)
        group(centred(mid2[...], m2[:, :rw] / count), next_to)

    result = products(early[...], (ow, far))
    for j, block in enumerate((1, 2)):
        by_block(info, block, 0, per, slots, sends, keep, result[j * rw : (j + 1) * rw])


def second_kernel(count, info, own_rows, near, m0, m1, ow, far, second, held):
    rw = own_rows.shape[1]

    @pl.when(info[MID] == 1)
    def _():
        second[...] = centred(near[...], m1[:, :rw] / count)

    @pl.when(info[MID] == 0)
    def _():
        second[...] = centred(own_rows[...], m0[:, :rw] / count)

    held[...] = products(second[...], (ow, far))


def first_chunk_kernel(start, second, far, wide, grads, right, held):
    weigh_kernel(start, far, wide, grads, right)
    held[...] = products(second[...], (right,))


def early_chunk_kernel(per, slots, info, early, right, keep, send):
    rw = early.shape[1] // 2
    result = products(early[...], (right,))
    for j, block in enumerate((1, 2)):
        by_block(info, block, 0, per, slots, (send,), keep, result[j * rw : (j + 1) * rw])


def late_kernel(
    count, per, slots,
    info, last1, last2, m2, m3, ow, far, chunk, held, held_chunk,
    keep, tile, *sends,
):
    rw = last1.shape[1]

    @pl.when(info[MID] == 1)
    def _():
        tile[...] = centred(last1[...], m2[:, :rw] / count)

    @pl.when(info[MID] == 0)
    def _():
        tile[...] = centred(last2[...], m3[:, :rw] / count)

    result = products(tile[...], (ow, far, chunk))
    before = jnp.concatenate((held[...], held_chunk[...]), axis=1)

    @functools.partial(low_or_high, info)
    def _(second_block, last_block):
        by_block(info, second_block, 0, per, slots, sends, keep, before)
        by_block(info, last_block, 0, per, slots, sends, keep, result)


def weigh_kernel(start, far, wide, grads, out):
    n, lanes = grads.shape[1], wide.shape[1]
    for a in range(0, n, lanes):
        cols = far[:, start + a : start + a + lanes]
        out[:, a : a + lanes] = weigh(wide[...], cols, grads[:, a : a + lanes])


def chunk_kernel(per, slots, info, early, second, last, right_ref, send, keep):
    rw = last.shape[1]
    right = right_ref[...]
    result = dot(right, early[...]).astype(BF)
    for j, block in enumerate((1, 2)):
        by_block(info, block, 1, per, slots, (send,), keep, result[:, j * rw : (j + 1) * rw])
    of_second = dot(right, second[...]).astype(BF)
    of_last = dot(right, last[...]).astype(BF)

    @functools.partial(low_or_high, info)
    def _(second_block, last_block):
        by_block(info, second_block, 1, per, slots, (send,), keep, of_second)
        by_block(info, last_block, 1, per, slots, (send,), keep, of_last)


def pair(keep, gots, i):
    start, values = 0, []
    for got in gots:
        width = got.shape[2]
        values.append(keep[i, :, start : start + width].astype(F32) + got[i].astype(F32))
        start += width
    return jnp.concatenate(values, axis=1)


def pair_kernel(first, pieces, count, cuts, info, keep, *refs):
    gots, outs = refs[:count], refs[count:]
    parts = len(cuts) - 1
    for k in range(len(outs) // parts):
        i = jnp.clip(info[TABLE + k + 1] - first, 0, pieces - 1)
        value = pair(keep, gots, i).astype(BF)
        for part in range(parts):
            outs[k * parts + part][...] = value[:, cuts[part] : cuts[part + 1]]


def total(keep, gots, others, i, cuts):
    parts = len(cuts) - 1
    value = pair(keep, gots, i)
    for k in range(len(others) // parts):
        got = [other[...] for other in others[k * parts : (k + 1) * parts]]
        value = value + jnp.concatenate(got, axis=1).astype(F32)
    return value


def gather_kernel(count, shapes, info, *refs):
    ham, corr = refs[-2:]
    cw = ham.shape[1] // 2
    pos = info[TABLE]

    def put(out, near, start, value):
        @pl.when((info[STRAIGHT] == 1) == near)
        def _():
            out[:, start : start + value.shape[1]] = value

        @pl.when((info[STRAIGHT] == 1) != near)
        def _():
            out[:, cw + start : cw + start + value.shape[1]] = value

    at = 0
    for n_gots, n_others, first, pieces, parts, cuts in shapes:
        keep, gots = refs[at], refs[at + 1 : at + 1 + n_gots]
        others = refs[at + 1 + n_gots : at + 1 + n_gots + n_others]
        at += 1 + n_gots + n_others

        @pl.when((pos >= first) & (pos < first + pieces))
        def _():
            value = total(keep, gots, others, pos - first, cuts) / count
            start = 0
            for got, (out, near, to) in zip(gots, parts):
                width = got.shape[2]
                put((ham, corr)[out], near, to, value[:, start : start + width])
                start += width


def last_kernel(count, shapes, info, held, *refs):
    del held
    out = refs[-1]
    at = start = 0
    for n_others, n in shapes:
        keep, got, *others = refs[at : at + 2 + n_others]
        at += 2 + n_others
        value = total(keep, (got,), others, info[TABLE], (0, keep.shape[2]))
        out[:, start : start + n] = value.T / count
        start += n


def last_chunks(count, start, info, ham, messages):
    rows, width = ham.shape
    shapes = [(len(others), keep.shape[1]) for keep, _, others, *_ in messages]
    flat = [a for keep, gots, others, *_ in messages for a in (keep, *gots, *others)]
    n = sum(s[1] for s in shapes)
    ahead, behind = (width // 2 + start) // n, start // n
    vmem = pl.BlockSpec(memory_space=pltpu.VMEM)
    return pl.pallas_call(
        functools.partial(last_kernel, count, shapes),
        out_shape=jax.ShapeDtypeStruct(ham.shape, ham.dtype),
        grid_spec=pltpu.PrefetchScalarGridSpec(
            num_scalar_prefetch=1,
            grid=(1,),
            in_specs=[pl.BlockSpec(memory_space=pl.ANY)] + [vmem] * len(flat),
            out_specs=pl.BlockSpec(
                (rows, n), lambda i, info: (0, jnp.where(info[STRAIGHT] == 1, ahead, behind))
            ),
        ),
        input_output_aliases={1: 0},
        compiler_params=pltpu.CompilerParams(vmem_limit_bytes=16 * 2**20),
        cost_estimate=pl.CostEstimate(flops=0, bytes_accessed=0, transcendentals=0),
    )(info, ham, *flat)


def per_device(o_rows, o_cols, grad_energy, energy):
    samples, rw = o_rows.shape
    cw = o_cols.shape[1]
    walkers = lax.axis_size("walker")
    chips = walkers // 2
    per = walkers // 4
    piece = rw // per
    w, y, z = (lax.axis_index(a) for a in ("walker", "prow", "pcol"))
    count = samples * walkers
    flip = [(0, 1), (1, 0)]
    outer = [(0, 1), (1, 0), (2, 3), (3, 2)]
    inner = [(1, 2), (2, 1)]
    ends = [(1, 0), (2, 3)]
    other_core = [(v, v ^ 1) for v in range(walkers)]

    order = [b * per + i for b in (1, 2, 0, 3) for i in range(per)]
    place = {v: [u for u in order if u % 2 == v % 2].index(v) for v in order}
    late_slots = {v: place[v] - per for v in order}
    table = [[place[(v + 2 * k) % walkers] for k in range(chips)] for v in range(walkers)]
    info = jnp.concatenate(
        (
            jnp.stack(((z == 1) | (z == 2), z < 2, w % 2, y == 0)).astype(jnp.int32),
            jnp.asarray(table, jnp.int32)[w],
        )
    )

    def shift(k, first, pieces):
        return [
            (v, (v + 2 * k) % walkers)
            for v in range(walkers)
            if first <= table[v][k] < first + pieces
        ]

    far_raw = lax.ppermute(o_cols, "prow", flip)
    near = lax.ppermute(o_rows, "pcol", outer)
    mid1 = lax.ppermute(o_rows, "pcol", inner)

    (sums,) = call(sums_kernel, [((1, rw + cw), F32)], o_rows, o_cols)
    m0 = lax.psum(sums, "walker")
    m1 = lax.ppermute(m0, "pcol", outer)
    m2 = lax.ppermute(m0, "pcol", [(0, 2), (1, 3), (2, 0), (3, 1)])

    column = energy[:, None]
    cuts = [0, cw // 2, 3 * cw // 4, cw]
    widths = [b - a for a, b in zip(cuts[:-1], cuts[1:])]
    ow, wide, *grads = call(
        functools.partial(own_kernel, count, cuts),
        [((samples, 2 * cw), BF), ((samples, min(widths)), F32)]
        + [((samples, n), BF) for n in widths],
        o_cols, grad_energy, column, m0,
    )

    near, mid1, m1, m2, ow, m0, *grads = lax.optimization_barrier(
        (near, mid1, m1, m2, ow, m0, *grads)
    )
    m3 = lax.ppermute(m0, "pcol", [(0, 3), (1, 2), (2, 1), (3, 0)])
    far_sums = lax.ppermute(m0, "prow", flip)
    mid2 = lax.ppermute(mid1, "pcol", ends)
    last1 = lax.ppermute(near, "pcol", inner)
    far_grads = [lax.ppermute(grads[0], "prow", flip)]

    (far_mean,) = call(
        functools.partial(mean_kernel, count), [((1, cw), F32)], far_sums, cost=MEAN_COST
    )
    (far,) = call(far_kernel, [((samples, cw), BF)], far_raw, far_mean, cost=FAR_COST)
    second, held = call(
        functools.partial(second_kernel, count),
        [((samples, rw), BF), ((rw, 3 * cw), BF)],
        info, o_rows, near, m0, m1, ow, far,
    )
    mid2, last1, far, m3, second, held, *grads = lax.optimization_barrier(
        (mid2, last1, far, m3, second, held, *grads)
    )
    last2 = lax.ppermute(last1, "pcol", ends)
    far_grads += [lax.ppermute(g, "prow", flip) for g in grads[1:]]

    messages = []

    def reduce(sends, keep, first, pieces, parts, split=None):
        width = keep.shape[2]
        at = (0, split, width) if split else (0, width)
        gots = [lax.ppermute(send, "walker", other_core) for send in sends]
        shapes = [((keep.shape[1], b - a), BF) for a, b in zip(at[:-1], at[1:])]
        sent = call(
            functools.partial(pair_kernel, first, pieces, len(gots), at),
            shapes * (chips - 1),
            info, keep, *gots,
        )
        others = [
            lax.ppermute(s, "walker", shift(i // len(shapes) + 1, first, pieces))
            for i, s in enumerate(sent)
        ]
        messages.append([keep, gots, others, first, pieces, parts, at])
        return sent

    parts = [(1, True, 0), (0, True, 0), (1, False, 0)]
    n = widths[0]
    message, short = ((per, piece, cw), BF), ((per, piece, n), BF)
    e_keep, early, *sends = call(
        functools.partial(early_kernel, count, per, place),
        [((per, piece, 3 * cw), BF), ((samples, 2 * rw), BF)] + [message] * 3,
        info, o_rows, near, mid1, mid2, m0, m1, m2, m3, ow, far,
    )
    reduce(sends, e_keep, 0, per, parts, 2 * cw)

    chunk, held_chunk = call(
        functools.partial(first_chunk_kernel, 0),
        [((samples, n), BF), ((rw, n), BF)],
        second, far, wide, far_grads[0],
        cost=FIRST_COST,
    )
    early_x = messages[0][2]
    last2, held_chunk, chunk, far_grads[1], *early_x = lax.optimization_barrier(
        (last2, held_chunk, chunk, far_grads[1], *early_x)
    )
    messages[0][2] = early_x
    l_keep, last, *sends = call(
        functools.partial(late_kernel, count, per, late_slots),
        [((per, piece, 3 * cw + n), BF), ((samples, rw), BF)] + [message] * 3 + [short],
        info, last1, last2, m2, m3, ow, far, chunk, held, held_chunk,
        cost=LAST_COST,
    )
    sent = reduce(sends, l_keep, per, per, parts + [(0, False, 0)])

    c_keep, send = call(
        functools.partial(early_chunk_kernel, per, place),
        [short, short],
        info, early, after(chunk, *sent),
    )
    reduce([send], c_keep, 0, per, [(0, False, 0)])

    for j in (1, 2):
        n = widths[j]
        (right,) = call(
            functools.partial(weigh_kernel, cuts[j]),
            [((samples, n), BF)],
            far, wide, far_grads[j],
            cost=WEIGH_COSTS[j],
        )
        send, keep = call(
            functools.partial(chunk_kernel, per, place),
            [((2 * per, n, piece), BF)] * 2,
            info, early, second, last, after(right, *sent),
        )
        sent = reduce([send], keep, 0, 2 * per, None)

    tail = messages[-2:]
    messages[0][0] = after(messages[0][0], *sent)
    flat, shapes = [], []
    for k, g, o, *what in messages[:-2]:
        flat += [k, *g, *o]
        shapes.append((len(g), len(o), *what))
    ham, corr = call(
        functools.partial(gather_kernel, count, shapes),
        [((piece, 2 * cw), F32)] * 2,
        info, *flat,
        cost=GATHER_COST,
    )
    return last_chunks(count, cuts[1], info, ham, tail), corr


def solution(mesh):
    in_specs = (
        P("walker", ("prow", "pcol")),
        P("walker", ("pcol", "prow")),
        P("walker", ("pcol", "prow")),
        P("walker"),
    )
    out_specs = (P(("prow", "walker"), "pcol"), P(("prow", "walker"), "pcol"))

    def per(*args):
        return tuple(per_device(*args))

    return jax.shard_map(
        per, mesh=mesh, in_specs=in_specs, out_specs=out_specs, check_vma=False
    )
```

```python
import functools

import jax
import jax.numpy as jnp
from jax import lax
from jax.experimental import pallas as pl
from jax.experimental.pallas import tpu as pltpu
from jax.sharding import PartitionSpec as P

BF = jnp.bfloat16
F32 = jnp.float32
VMEM = pl.BlockSpec(memory_space=pltpu.VMEM)
SMEM = pl.BlockSpec(memory_space=pltpu.SMEM)
MID, LOW, CORE, STRAIGHT, TABLE = 0, 1, 2, 3, 4
MEAN_COST, FAR_COST, EARLY_COST, FIRST_COST, LAST_COST = 6, 3, 4, 0, 4
WEIGH_COST, FOLD_COST = 12, 6


def call(kernel, outs, *args, scratch=(), limit=24, cost=0):
    return pl.pallas_call(
        kernel,
        out_shape=[jax.ShapeDtypeStruct(s, d) for s, d in outs],
        in_specs=[SMEM if a.dtype == jnp.int32 else VMEM for a in args],
        out_specs=[VMEM] * len(outs),
        scratch_shapes=list(scratch),
        compiler_params=pltpu.CompilerParams(vmem_limit_bytes=limit * 2**20),
        cost_estimate=pl.CostEstimate(
            flops=int(cost * 1.15e9), bytes_accessed=0, transcendentals=0
        ),
    )(*args)


def after(value, *others):
    return lax.optimization_barrier((value,) + others)[0]


def centred(values, mean):
    return (values.astype(F32) - mean).astype(BF)


def weigh(energy, cols, grads):
    return (energy * cols.astype(F32) + grads.astype(F32)).astype(BF)


def dot(rows, right):
    return lax.dot_general(rows, right, (((0,), (0,)), ((), ())), preferred_element_type=F32)


def sums_kernel(rows, cols, out):
    width = rows.shape[1]
    out[:, :width] = jnp.sum(rows[...].astype(F32), axis=0, keepdims=True)
    out[:, width:] = jnp.sum(cols[...].astype(F32), axis=0, keepdims=True)


def own_kernel(count, cuts, cols, grads, energy, sums, out, wide, *pieces):
    width = cols.shape[1]
    lanes = wide.shape[1]
    d = centred(cols[...], sums[:, -width:] / count)
    out[:, :width] = d
    spread = jnp.broadcast_to(energy[...], wide.shape)
    wide[...] = spread
    for a in range(0, width, lanes):
        b = a + lanes
        out[:, width + a : width + b] = weigh(spread, d[:, a:b], grads[:, a:b])
    for a, b, piece in zip(cuts[:-1], cuts[1:], pieces):
        piece[...] = grads[:, a:b]


def by_core(info, walker, slot, sends, keep, value, turn=None):
    width = value.shape[-1]
    turn = width if turn is None else turn
    for core in (0, 1):

        @pl.when(info[CORE] == core)
        def _():
            for a, b, kept in ((0, turn, core == walker % 2), (turn, width, core != walker % 2)):
                if kept and a < b:
                    keep[slot, :, a:b] = value[:, a:b]
                start = 0
                for send in sends:
                    lo, hi = max(a, start), min(b, start + send.shape[-1])
                    if not kept and lo < hi:
                        send[slot, :, lo - start : hi - start] = value[:, lo:hi]
                    start += send.shape[-1]


def products(tile, rights):
    return jnp.concatenate([dot(tile, right[...]).astype(BF) for right in rights], axis=1)


def by_block(info, block, axis, per, slots, sends, keep, value):
    piece = value.shape[axis] // per
    turn = value.shape[1] // 2 if axis == 0 and per == 1 else None
    for i in range(per):
        at = slice(i * piece, (i + 1) * piece)
        walker = block * per + i
        part = value[at] if axis == 0 else value[:, at]
        by_core(info, walker, slots[walker], sends, keep, part, turn)


def low_or_high(info, then):
    for low in (1, 0):
        pl.when(info[LOW] == low)(functools.partial(then, 0 if low else 3, 3 if low else 0))


def mean_kernel(count, sums, m1, m2, out, near_mean, next_mean):
    rw = near_mean.shape[1]
    out[...] = sums[:, -out.shape[1] :] / count
    near_mean[...] = m1[:, :rw] / count
    next_mean[...] = m2[:, :rw] / count


def far_kernel(raw, mean, out):
    out[...] = centred(raw[...], mean[...])


def early_kernel(
    count, per, slots,
    info, own_rows, near, mid1, mid2, m0, m1, m2, m3, ow, far,
    keep, early, *sends,
):
    rw = own_rows.shape[1]

    def group(there, beside):
        @pl.when(info[LOW] == 1)
        def _():
            early[:, rw:] = there
            early[:, :rw] = beside

        @pl.when(info[LOW] == 0)
        def _():
            early[:, :rw] = there
            early[:, rw:] = beside

    @pl.when(info[MID] == 1)
    def _():
        own = centred(own_rows[...], m0[:, :rw] / count)
        group(centred(mid1[...], m3[:, :rw] / count), own)

    @pl.when(info[MID] == 0)
    def _():
        next_to = centred(near[...], m1[...])
        group(centred(mid2[...], m2[...]), next_to)

    result = products(early[...], (ow, far))
    for j, block in enumerate((1, 2)):
        by_block(info, block, 0, per, slots, sends, keep, result[j * rw : (j + 1) * rw])


def second_kernel(count, info, own_rows, near, m0, m1, ow, far, second, held):
    rw = own_rows.shape[1]

    @pl.when(info[MID] == 1)
    def _():
        second[...] = centred(near[...], m1[...])

    @pl.when(info[MID] == 0)
    def _():
        second[...] = centred(own_rows[...], m0[:, :rw] / count)

    held[...] = products(second[...], (ow, far))


def first_chunk_kernel(start, second, far, wide, grads, right, held):
    weigh_kernel(start, far, wide, grads, right)
    held[...] = products(second[...], (right,))


def early_chunk_kernel(per, slots, info, early, right, keep, send):
    rw = early.shape[1] // 2
    result = products(early[...], (right,))
    for j, block in enumerate((1, 2)):
        by_block(info, block, 0, per, slots, (send,), keep, result[j * rw : (j + 1) * rw])


def late_kernel(
    count, per, slots,
    info, last1, last2, m2, m3, ow, far, chunk, held, held_chunk,
    keep, tile, *sends,
):
    rw = last1.shape[1]

    @pl.when(info[MID] == 1)
    def _():
        tile[...] = centred(last1[...], m2[...])

    @pl.when(info[MID] == 0)
    def _():
        tile[...] = centred(last2[...], m3[:, :rw] / count)

    result = products(tile[...], (ow, far, chunk))
    before = jnp.concatenate((held[...], held_chunk[...]), axis=1)

    @functools.partial(low_or_high, info)
    def _(second_block, last_block):
        by_block(info, second_block, 0, per, slots, sends, keep, before)
        by_block(info, last_block, 0, per, slots, sends, keep, result)


def weigh_kernel(start, far, wide, grads, out):
    n, lanes = grads.shape[1], wide.shape[1]
    for a in range(0, n, lanes):
        cols = far[:, start + a : start + a + lanes]
        out[:, a : a + lanes] = weigh(wide[...], cols, grads[:, a : a + lanes])


def chunk_kernel(per, slots, info, early, second, last, right_ref, send, keep):
    rw = last.shape[1]
    right = right_ref[...]
    result = dot(right, early[...]).astype(BF)
    for j, block in enumerate((1, 2)):
        by_block(info, block, 1, per, slots, (send,), keep, result[:, j * rw : (j + 1) * rw])
    of_second = dot(right, second[...]).astype(BF)
    of_last = dot(right, last[...]).astype(BF)

    @functools.partial(low_or_high, info)
    def _(second_block, last_block):
        by_block(info, second_block, 1, per, slots, (send,), keep, of_second)
        by_block(info, last_block, 1, per, slots, (send,), keep, of_last)


def pair(keep, gots, i):
    start, values = 0, []
    for got in gots:
        width = got.shape[2]
        values.append(keep[i, :, start : start + width].astype(F32) + got[i].astype(F32))
        start += width
    return jnp.concatenate(values, axis=1)


def pair_kernel(first, pieces, count, info, keep, *refs):
    gots, outs = refs[:count], refs[count:]
    for k, out in enumerate(outs, 1):
        i = jnp.clip(info[TABLE + k] - first, 0, pieces - 1)
        out[...] = pair(keep, gots, i).astype(BF)


def total(keep, gots, others, i):
    value = pair(keep, gots, i)
    for other in others:
        value = value + other[...].astype(F32)
    return value


def columns(keep, gots, lo, hi):
    start, values = 0, []
    for got in gots:
        a, b = max(lo, start), min(hi, start + got.shape[2])
        if a < b:
            values.append(keep[0, :, a:b].astype(F32) + got[0, :, a - start : b - start].astype(F32))
        start += got.shape[2]
    return jnp.concatenate(values, axis=1)


def away_kernel(first, count, info, keep, *refs):
    gots, out = refs[:count], refs[count]
    width = keep.shape[2]

    @pl.when(info[TABLE] == first)
    def _():
        out[...] = columns(keep, gots, width // 2, width).astype(BF)

    @pl.when(info[TABLE] != first)
    def _():
        out[...] = columns(keep, gots, 0, width // 2).astype(BF)


def home_kernel(count, info, keep, *refs):
    gots, got_x, outs = refs[:count], refs[count], refs[count + 1 :]
    width = keep.shape[2]
    value = (columns(keep, gots, width // 2, width) + got_x[...].astype(F32)).astype(BF)
    start = 0
    for out in outs:
        out[...] = value[:, start : start + out.shape[1]]
        start += out.shape[1]


def fold_kernel(count, info, keep, got, *refs):
    refs[-1][...] = total(keep, (got,), refs[:-1], info[TABLE]).T / count


def gather_kernel(count, shapes, info, *refs):
    *refs, chunk, ham, corr = refs
    cw = ham.shape[1] // 2
    pos = info[TABLE]

    def put(out, near, start, value):
        @pl.when((info[STRAIGHT] == 1) == near)
        def _():
            out[:, start : start + value.shape[1]] = value

        @pl.when((info[STRAIGHT] == 1) != near)
        def _():
            out[:, cw + start : cw + start + value.shape[1]] = value

    def spans(refs, start=0):
        for ref in refs:
            yield start, start + ref.shape[-1], ref
            start += ref.shape[-1]

    put(ham, False, cw - chunk.shape[1], chunk[...])
    at = 0
    for n_gots, n_others, turned, first, pieces, parts in shapes:
        keep, gots = refs[at], refs[at + 1 : at + 1 + n_gots]
        others = refs[at + 1 + n_gots : at + 1 + n_gots + n_others]
        at += 1 + n_gots + n_others
        width = keep.shape[2]

        def place(a, b, value):
            start = 0
            for size, (out, near, to) in parts:
                lo, hi = max(a, start), min(b, start + size)
                if lo < hi:
                    put((ham, corr)[out], near, to + lo - start, value[:, lo - a : hi - a] / count)
                start += size

        @pl.when((pos >= first) & (pos < first + pieces))
        def _():
            i = pos - first
            for a, b, got in spans(gots):
                b = min(b, width // 2) if turned else b
                if a < b:
                    value = keep[i, :, a:b].astype(F32) + got[i, :, : b - a].astype(F32)
                    for other in others[:1] if turned else others:
                        value = value + other[:, a:b].astype(F32)
                    place(a, b, value)
            if turned:
                for a, b, home in spans(others[1:], width // 2):
                    place(a, b, home[...].astype(F32))


def per_device(o_rows, o_cols, grad_energy, energy):
    samples, rw = o_rows.shape
    cw = o_cols.shape[1]
    walkers = lax.axis_size("walker")
    chips = walkers // 2
    per = walkers // 4
    piece = rw // per
    w, y, z = (lax.axis_index(a) for a in ("walker", "prow", "pcol"))
    count = samples * walkers
    flip = [(0, 1), (1, 0)]
    outer = [(0, 1), (1, 0), (2, 3), (3, 2)]
    inner = [(1, 2), (2, 1)]
    ends = [(1, 0), (2, 3)]
    other_core = [(v, v ^ 1) for v in range(walkers)]

    order = [b * per + i for b in (1, 2, 0, 3) for i in range(per)]
    place = {v: [u for u in order if u % 2 == v % 2].index(v) for v in order}
    late_slots = {v: place[v] - per for v in order}
    table = [[place[(v + 2 * k) % walkers] for k in range(chips)] for v in range(walkers)]
    info = jnp.concatenate(
        (
            jnp.stack(((z == 1) | (z == 2), z < 2, w % 2, y == 0)).astype(jnp.int32),
            jnp.asarray(table, jnp.int32)[w],
        )
    )

    def shift(k, first, pieces):
        return [
            (v, (v + 2 * k) % walkers)
            for v in range(walkers)
            if first <= table[v][k] < first + pieces
        ]

    far_raw = lax.ppermute(o_cols, "prow", flip)
    near = lax.ppermute(o_rows, "pcol", outer)
    mid1 = lax.ppermute(o_rows, "pcol", inner)

    (sums,) = call(sums_kernel, [((1, rw + cw), F32)], o_rows, o_cols)
    m0 = lax.psum(sums, "walker")
    m1 = lax.ppermute(m0, "pcol", outer)
    m2 = lax.ppermute(m0, "pcol", [(0, 2), (1, 3), (2, 0), (3, 1)])

    column = energy[:, None]
    cuts = [0, cw // 2, cw]
    widths = [b - a for a, b in zip(cuts[:-1], cuts[1:])]
    ow, wide, *grads = call(
        functools.partial(own_kernel, count, cuts),
        [((samples, 2 * cw), BF), ((samples, min(widths)), F32)]
        + [((samples, n), BF) for n in widths],
        o_cols, grad_energy, column, m0,
    )

    near, mid1, ow, m0, *grads = lax.optimization_barrier((near, mid1, ow, m0, *grads))
    m3 = lax.ppermute(m0, "pcol", [(0, 3), (1, 2), (2, 1), (3, 0)])
    far_sums = lax.ppermute(m0, "prow", flip)
    mid2 = lax.ppermute(mid1, "pcol", ends)
    last1 = lax.ppermute(near, "pcol", inner)
    far_grads = [lax.ppermute(grads[0], "prow", flip)]

    far_mean, m1, m2 = call(
        functools.partial(mean_kernel, count),
        [((1, cw), F32), ((1, rw), F32), ((1, rw), F32)],
        far_sums, m1, m2,
        cost=MEAN_COST,
    )
    (far,) = call(far_kernel, [((samples, cw), BF)], far_raw, far_mean, cost=FAR_COST)
    second, held = call(
        functools.partial(second_kernel, count),
        [((samples, rw), BF), ((rw, 3 * cw), BF)],
        info, o_rows, near, m0, m1, ow, far,
    )
    last1, far, m3, second, held, *grads = lax.optimization_barrier(
        (last1, far, m3, second, held, *grads)
    )
    last2 = lax.ppermute(last1, "pcol", ends)
    far_grads += [lax.ppermute(g, "prow", flip) for g in grads[1:]]

    messages = []

    def reduce(sends, keep, first, pieces, parts):
        gots = [lax.ppermute(send, "walker", other_core) for send in sends]
        sent = call(
            functools.partial(pair_kernel, first, pieces, len(gots)),
            [(keep.shape[1:], BF)] * (chips - 1),
            info, keep, *gots,
        )
        others = [
            lax.ppermute(s, "walker", shift(k, first, pieces)) for k, s in enumerate(sent, 1)
        ]
        messages.append([keep, gots, others, False, first, pieces, parts])
        return sent

    def reduce_rows(sends, keep, first, parts):
        if per > 1:
            return reduce(sends, keep, first, per, parts)
        gots = [lax.ppermute(send, "walker", other_core) for send in sends]
        shape = (keep.shape[1], keep.shape[2] // 2)
        sent = call(
            functools.partial(away_kernel, first, len(gots)), [(shape, BF)], info, keep, *gots
        )
        got_x = lax.ppermute(sent[0], "walker", [(v, v ^ 2) for v in range(4)])
        messages.append([keep, gots, [got_x], True, first, 1, parts])
        return sent

    def bring_home(message, sizes, *earlier):
        keep, gots, others, turned, *_ = message
        if turned:
            homes = call(
                functools.partial(home_kernel, len(gots)),
                [((keep.shape[1], size), BF) for size in sizes],
                info, keep, *gots, after(others[0], *earlier),
            )
            others += [lax.ppermute(h, "walker", other_core) for h in homes]

    n = widths[0]
    parts = [(cw, (1, True, 0)), (cw, (0, True, 0)), (cw, (1, False, 0))]
    chunk_part = [(n, (0, False, 0))]

    def message_shapes(*sizes):
        return [((per, piece, size), BF) for size in sizes]

    e_keep, early, *sends = call(
        functools.partial(early_kernel, count, per, place),
        message_shapes(3 * cw) + [((samples, 2 * rw), BF)] + message_shapes(*[3 * cw // 4] * 4),
        info, o_rows, near, mid1, mid2, m0, m1, m2, m3, ow, far,
        cost=EARLY_COST,
    )
    reduce_rows(sends, e_keep, 0, parts)

    chunk, held_chunk = call(
        functools.partial(first_chunk_kernel, 0),
        [((samples, n), BF), ((rw, n), BF)],
        second, far, wide, far_grads[0],
        cost=FIRST_COST,
    )
    c_keep, send = call(
        functools.partial(early_chunk_kernel, per, place), message_shapes(n, n), info, early, chunk
    )
    reduce_rows([send], c_keep, 0, chunk_part)

    last2, held_chunk, chunk, messages[0][2], messages[1][2] = lax.optimization_barrier(
        (last2, held_chunk, chunk, messages[0][2], messages[1][2])
    )
    size = (3 * cw + n) // 2
    l_keep, last, *sends = call(
        functools.partial(late_kernel, count, per, late_slots),
        message_shapes(2 * size) + [((samples, rw), BF)] + message_shapes(*[cw, size - cw] * 2),
        info, last1, last2, m2, m3, ow, far, chunk, held, held_chunk,
        cost=LAST_COST,
    )
    sent = reduce_rows(sends, l_keep, per, parts + chunk_part)

    bring_home(messages[0], [3 * cw // 2], *sent)
    bring_home(messages[1], [n // 2], *sent)
    n = widths[1]
    (right,) = call(
        functools.partial(weigh_kernel, cuts[1]),
        [((samples, n), BF)],
        far, wide, far_grads[1],
        cost=WEIGH_COST,
    )
    messages[0][2], messages[1][2], right = lax.optimization_barrier(
        (messages[0][2], messages[1][2], right)
    )
    send, keep = call(
        functools.partial(chunk_kernel, per, place),
        [((2 * per, n, piece), BF)] * 2,
        info, early, second, last, after(right, *sent),
    )
    sent = reduce([send], keep, 0, 2 * per, None)
    keep, gots, others, *_ = messages.pop()
    (folded,) = call(
        functools.partial(fold_kernel, count),
        [((piece, n), F32)],
        info, keep, *gots, *others,
        cost=FOLD_COST,
    )
    bring_home(messages[2], [min(256, size - a) for a in range(0, size, 256)], *sent)

    flat, shapes = [], []
    for k, g, o, *what in messages:
        flat += [k, *g, *o]
        shapes.append((len(g), len(o), *what))
    return call(
        functools.partial(gather_kernel, count, shapes),
        [((piece, 2 * cw), F32)] * 2,
        info, *flat, folded,
    )


def solution(mesh):
    in_specs = (
        P("walker", ("prow", "pcol")),
        P("walker", ("pcol", "prow")),
        P("walker", ("pcol", "prow")),
        P("walker"),
    )
    out_specs = (P(("prow", "walker"), "pcol"), P(("prow", "walker"), "pcol"))

    def per(*args):
        return tuple(per_device(*args))

    return jax.shard_map(
        per, mesh=mesh, in_specs=in_specs, out_specs=out_specs, check_vma=False
    )
```

```python
import functools

import jax
import jax.numpy as jnp
from jax import lax
from jax.experimental import pallas as pl
from jax.experimental.pallas import tpu as pltpu
from jax.sharding import PartitionSpec as P

BF = jnp.bfloat16
F32 = jnp.float32
VMEM = pl.BlockSpec(memory_space=pltpu.VMEM)
SMEM = pl.BlockSpec(memory_space=pltpu.SMEM)
MID, LOW, CORE, STRAIGHT, TABLE = 0, 1, 2, 3, 4
MEAN_COST, FAR_COST, EARLY_COST, FIRST_COST, LAST_COST = 6, 3, 4, 0, 4
WEIGH_COST, HOPS = 12, 4


def call(kernel, outs, *args, scratch=(), limit=24, cost=0, out_spec=VMEM):
    return pl.pallas_call(
        kernel,
        out_shape=[jax.ShapeDtypeStruct(s, d) for s, d in outs],
        in_specs=[SMEM if a.dtype == jnp.int32 else VMEM for a in args],
        out_specs=[out_spec] * len(outs),
        scratch_shapes=list(scratch),
        compiler_params=pltpu.CompilerParams(vmem_limit_bytes=limit * 2**20),
        cost_estimate=pl.CostEstimate(
            flops=int(cost * 1.15e9), bytes_accessed=0, transcendentals=0
        ),
    )(*args)


def after(value, *others):
    return lax.optimization_barrier((value,) + others)[0]


def centred(values, mean):
    return (values.astype(F32) - mean).astype(BF)


def weigh(energy, cols, grads):
    return (energy * cols.astype(F32) + grads.astype(F32)).astype(BF)


def dot(rows, right):
    return lax.dot_general(rows, right, (((0,), (0,)), ((), ())), preferred_element_type=F32)


def sums_kernel(rows, cols, out):
    width = rows.shape[1]
    out[:, :width] = jnp.sum(rows[...].astype(F32), axis=0, keepdims=True)
    out[:, width:] = jnp.sum(cols[...].astype(F32), axis=0, keepdims=True)


def own_kernel(count, cuts, cols, grads, energy, sums, out, wide, *pieces):
    width = cols.shape[1]
    lanes = wide.shape[1]
    d = centred(cols[...], sums[:, -width:] * (1 / count))
    out[:, :width] = d
    spread = jnp.broadcast_to(energy[...], wide.shape)
    wide[...] = spread
    for a in range(0, width, lanes):
        b = a + lanes
        out[:, width + a : width + b] = weigh(spread, d[:, a:b], grads[:, a:b])
    for a, b, piece in zip(cuts[:-1], cuts[1:], pieces):
        piece[...] = grads[:, a:b]


def by_core(info, walker, slot, sends, keep, value, turn=None):
    width = value.shape[-1]
    turn = width if turn is None else turn
    for core in (0, 1):

        @pl.when(info[CORE] == core)
        def _():
            for a, b, kept in ((0, turn, core == walker % 2), (turn, width, core != walker % 2)):
                if kept and a < b:
                    keep[slot, :, a:b] = value[:, a:b]
                start = 0
                for send in sends:
                    lo, hi = max(a, start), min(b, start + send.shape[-1])
                    if not kept and lo < hi:
                        send[slot, :, lo - start : hi - start] = value[:, lo:hi]
                    start += send.shape[-1]


def products(tile, rights):
    return jnp.concatenate([dot(tile, right[...]).astype(BF) for right in rights], axis=1)


def by_block(info, block, axis, per, slots, sends, keep, value):
    piece = value.shape[axis] // per
    turn = value.shape[1] // 2 if axis == 0 and per == 1 else None
    for i in range(per):
        at = slice(i * piece, (i + 1) * piece)
        walker = block * per + i
        part = value[at] if axis == 0 else value[:, at]
        by_core(info, walker, slots[walker], sends, keep, part, turn)


def low_or_high(info, then):
    for low in (1, 0):
        pl.when(info[LOW] == low)(functools.partial(then, 0 if low else 3, 3 if low else 0))


def mean_kernel(count, sums, m1, m2, out, near_mean, next_mean):
    rw = near_mean.shape[1]
    out[...] = sums[:, -out.shape[1] :] * (1 / count)
    near_mean[...] = m1[:, :rw] * (1 / count)
    next_mean[...] = m2[:, :rw] * (1 / count)


def far_kernel(raw, mean, out):
    out[...] = centred(raw[...], mean[...])


def early_kernel(
    count, per, slots,
    info, own_rows, near, mid1, mid2, m0, m1, m2, m3, ow, far,
    keep, early, *sends,
):
    rw = own_rows.shape[1]

    def group(there, beside):
        @pl.when(info[LOW] == 1)
        def _():
            early[:, rw:] = there
            early[:, :rw] = beside

        @pl.when(info[LOW] == 0)
        def _():
            early[:, :rw] = there
            early[:, rw:] = beside

    @pl.when(info[MID] == 1)
    def _():
        own = centred(own_rows[...], m0[:, :rw] * (1 / count))
        group(centred(mid1[...], m3[:, :rw] * (1 / count)), own)

    @pl.when(info[MID] == 0)
    def _():
        next_to = centred(near[...], m1[...])
        group(centred(mid2[...], m2[...]), next_to)

    result = products(early[...], (ow, far))
    for j, block in enumerate((1, 2)):
        by_block(info, block, 0, per, slots, sends, keep, result[j * rw : (j + 1) * rw])


def second_kernel(count, info, own_rows, near, m0, m1, ow, far, second, held):
    rw = own_rows.shape[1]

    @pl.when(info[MID] == 1)
    def _():
        second[...] = centred(near[...], m1[...])

    @pl.when(info[MID] == 0)
    def _():
        second[...] = centred(own_rows[...], m0[:, :rw] * (1 / count))

    held[...] = products(second[...], (ow, far))


def first_chunk_kernel(start, second, far, wide, grads, right, held):
    weigh_kernel(start, far, wide, grads, right)
    held[...] = products(second[...], (right,))


def early_chunk_kernel(per, slots, info, early, right, keep, send):
    rw = early.shape[1] // 2
    result = products(early[...], (right,))
    for j, block in enumerate((1, 2)):
        by_block(info, block, 0, per, slots, (send,), keep, result[j * rw : (j + 1) * rw])


def late_kernel(
    count, per, slots,
    info, last1, last2, m2, m3, ow, far, chunk, held, held_chunk,
    keep, tile, *sends,
):
    rw = last1.shape[1]

    @pl.when(info[MID] == 1)
    def _():
        tile[...] = centred(last1[...], m2[...])

    @pl.when(info[MID] == 0)
    def _():
        tile[...] = centred(last2[...], m3[:, :rw] * (1 / count))

    result = products(tile[...], (ow, far, chunk))
    before = jnp.concatenate((held[...], held_chunk[...]), axis=1)

    @functools.partial(low_or_high, info)
    def _(second_block, last_block):
        by_block(info, second_block, 0, per, slots, sends, keep, before)
        by_block(info, last_block, 0, per, slots, sends, keep, result)


def weigh_kernel(start, far, wide, grads, out):
    n, lanes = grads.shape[1], wide.shape[1]
    for a in range(0, n, lanes):
        cols = far[:, start + a : start + a + lanes]
        out[:, a : a + lanes] = weigh(wide[...], cols, grads[:, a : a + lanes])


def chunk_kernel(per, slots, info, early, second, last, right_ref, send, keep):
    rw = last.shape[1]
    right = right_ref[...]
    result = dot(right, early[...]).astype(BF)
    for j, block in enumerate((1, 2)):
        by_block(info, block, 1, per, slots, (send,), keep, result[:, j * rw : (j + 1) * rw])
    of_second = dot(right, second[...]).astype(BF)
    of_last = dot(right, last[...]).astype(BF)

    @functools.partial(low_or_high, info)
    def _(second_block, last_block):
        by_block(info, second_block, 1, per, slots, (send,), keep, of_second)
        by_block(info, last_block, 1, per, slots, (send,), keep, of_last)


def pair(keep, gots, i):
    start, values = 0, []
    for got in gots:
        width = got.shape[2]
        values.append(keep[i, :, start : start + width].astype(F32) + got[i].astype(F32))
        start += width
    return jnp.concatenate(values, axis=1)


def pair_kernel(first, pieces, count, info, keep, *refs):
    gots, outs = refs[:count], refs[count:]
    for k, out in enumerate(outs, 1):
        i = jnp.clip(info[TABLE + k] - first, 0, pieces - 1)
        out[...] = pair(keep, gots, i).astype(BF)


def total(keep, gots, others, i):
    value = pair(keep, gots, i)
    for other in others:
        value = value + other[...].astype(F32)
    return value


def columns(keep, gots, lo, hi):
    start, values = 0, []
    for got in gots:
        a, b = max(lo, start), min(hi, start + got.shape[2])
        if a < b:
            values.append(keep[0, :, a:b].astype(F32) + got[0, :, a - start : b - start].astype(F32))
        start += got.shape[2]
    return jnp.concatenate(values, axis=1)


def away_kernel(first, count, info, keep, *refs):
    gots, out = refs[:count], refs[count]
    width = keep.shape[2]

    @pl.when(info[TABLE] == first)
    def _():
        out[...] = columns(keep, gots, width // 2, width).astype(BF)

    @pl.when(info[TABLE] != first)
    def _():
        out[...] = columns(keep, gots, 0, width // 2).astype(BF)


def home_kernel(count, info, keep, *refs):
    gots, got_x, outs = refs[:count], refs[count], refs[count + 1 :]
    width = keep.shape[2]
    value = (columns(keep, gots, width // 2, width) + got_x[...].astype(F32)).astype(BF)
    rows = value.shape[0] // len(outs)
    for i, out in enumerate(outs):
        out[...] = value[i * rows : (i + 1) * rows]


def gather_kernel(count, shapes, info, *refs):
    *refs, ham_out, corr_out, ham, corr, sems = refs
    rows, cw = ham.shape[0], ham.shape[1] // 2
    pos = info[TABLE]
    step = rows // HOPS

    def put(out, near, at, start, value):
        @pl.when((info[STRAIGHT] == 1) == near)
        def _():
            out[at, start : start + value.shape[1]] = value

        @pl.when((info[STRAIGHT] == 1) != near)
        def _():
            out[at, cw + start : cw + start + value.shape[1]] = value

    def spans(refs, start=0):
        for ref in refs:
            yield start, start + ref.shape[-1], ref
            start += ref.shape[-1]

    def place(parts, at, a, b, value):
        start = 0
        for size, (out, near, to) in parts:
            lo, hi = max(a, start), min(b, start + size)
            if lo < hi:
                some = value[:, lo - a : hi - a] * (1 / count)
                put((ham, corr)[out], near, at, to + lo - start, some)
            start += size

    def fill(k, keep, gots, others, turned, i, parts):
        at, width = slice(k * step, (k + 1) * step), keep.shape[2]
        for a, b, got in spans(gots):
            b = min(b, width // 2) if turned else b
            if a < b:
                value = keep[i, at, a:b].astype(F32) + got[i, at, : b - a].astype(F32)
                for other in others[:1] if turned else others:
                    value = value + other[at, a:b].astype(F32)
                place(parts, at, a, b, value)
        if turned:
            homes = others[1:]
            home = homes[k * len(homes) // HOPS]
            start = k * step % home.shape[0]
            place(parts, at, width // 2, width, home[start : start + step].astype(F32))

    def copies(k):
        at = slice(k * step, (k + 1) * step)
        return [
            pltpu.make_async_copy(ham.at[at], ham_out.at[at], sems.at[k, 0]),
            pltpu.make_async_copy(corr.at[at], corr_out.at[at], sems.at[k, 1]),
        ]

    start, messages = 0, []
    for n_gots, n_others, turned, first, pieces, parts in shapes:
        keep, gots = refs[start], refs[start + 1 : start + 1 + n_gots]
        others = refs[start + 1 + n_gots : start + 1 + n_gots + n_others]
        start += 1 + n_gots + n_others
        if parts[0][0] is None:
            out, near, to = parts[0][1]
            value = total(keep, gots, others, pos).T * (1 / count)
            put((ham, corr)[out], near, slice(None), to, value)
        else:
            messages.append((first, pieces, keep, gots, others, turned, parts))
    for k in range(HOPS):
        for first, pieces, keep, gots, others, turned, parts in messages:

            @pl.when((pos >= first) & (pos < first + pieces))
            def _():
                fill(k, keep, gots, others, turned, pos - first, parts)

        for copy in copies(k):
            copy.start()
    for k in range(HOPS):
        for copy in copies(k):
            copy.wait()


def per_device(o_rows, o_cols, grad_energy, energy):
    samples, rw = o_rows.shape
    cw = o_cols.shape[1]
    walkers = lax.axis_size("walker")
    chips = walkers // 2
    per = walkers // 4
    piece = rw // per
    w, y, z = (lax.axis_index(a) for a in ("walker", "prow", "pcol"))
    count = samples * walkers
    flip = [(0, 1), (1, 0)]
    outer = [(0, 1), (1, 0), (2, 3), (3, 2)]
    inner = [(1, 2), (2, 1)]
    ends = [(1, 0), (2, 3)]
    other_core = [(v, v ^ 1) for v in range(walkers)]

    order = [b * per + i for b in (1, 2, 0, 3) for i in range(per)]
    place = {v: [u for u in order if u % 2 == v % 2].index(v) for v in order}
    late_slots = {v: place[v] - per for v in order}
    table = [[place[(v + 2 * k) % walkers] for k in range(chips)] for v in range(walkers)]
    info = jnp.concatenate(
        (
            jnp.stack(((z == 1) | (z == 2), z < 2, w % 2, y == 0)).astype(jnp.int32),
            jnp.asarray(table, jnp.int32)[w],
        )
    )

    def shift(k, first, pieces):
        return [
            (v, (v + 2 * k) % walkers)
            for v in range(walkers)
            if first <= table[v][k] < first + pieces
        ]

    far_raw = lax.ppermute(o_cols, "prow", flip)
    near = lax.ppermute(o_rows, "pcol", outer)
    mid1 = lax.ppermute(o_rows, "pcol", inner)

    (sums,) = call(sums_kernel, [((1, rw + cw), F32)], o_rows, o_cols)
    m0 = lax.psum(sums, "walker")
    m1 = lax.ppermute(m0, "pcol", outer)
    m2 = lax.ppermute(m0, "pcol", [(0, 2), (1, 3), (2, 0), (3, 1)])

    column = energy[:, None]
    cuts = [0, cw // 2, cw]
    widths = [b - a for a, b in zip(cuts[:-1], cuts[1:])]
    ow, wide, *grads = call(
        functools.partial(own_kernel, count, cuts),
        [((samples, 2 * cw), BF), ((samples, min(widths)), F32)]
        + [((samples, n), BF) for n in widths],
        o_cols, grad_energy, column, m0,
    )

    near, mid1, m1, ow, m0, *grads = lax.optimization_barrier((near, mid1, m1, ow, m0, *grads))
    m3 = lax.ppermute(m0, "pcol", [(0, 3), (1, 2), (2, 1), (3, 0)])
    far_sums = lax.ppermute(m0, "prow", flip)
    mid2 = lax.ppermute(mid1, "pcol", ends)
    last1 = lax.ppermute(near, "pcol", inner)
    far_grads = [lax.ppermute(grads[0], "prow", flip)]

    far_mean, m1, m2 = call(
        functools.partial(mean_kernel, count),
        [((1, cw), F32), ((1, rw), F32), ((1, rw), F32)],
        far_sums, m1, m2,
        cost=MEAN_COST,
    )
    (far,) = call(far_kernel, [((samples, cw), BF)], far_raw, far_mean, cost=FAR_COST)
    second, held = call(
        functools.partial(second_kernel, count),
        [((samples, rw), BF), ((rw, 3 * cw), BF)],
        info, o_rows, near, m0, m1, ow, far,
    )
    last1, far, m3, second, held, *grads = lax.optimization_barrier(
        (last1, far, m3, second, held, *grads)
    )
    last2 = lax.ppermute(last1, "pcol", ends)
    far_grads += [lax.ppermute(g, "prow", flip) for g in grads[1:]]

    messages = []

    def reduce(sends, keep, first, pieces, parts):
        gots = [lax.ppermute(send, "walker", other_core) for send in sends]
        sent = call(
            functools.partial(pair_kernel, first, pieces, len(gots)),
            [(keep.shape[1:], BF)] * (chips - 1),
            info, keep, *gots,
        )
        others = [
            lax.ppermute(s, "walker", shift(k, first, pieces)) for k, s in enumerate(sent, 1)
        ]
        messages.append([keep, gots, others, False, first, pieces, parts])
        return sent

    def reduce_rows(sends, keep, first, parts):
        if per > 1:
            return reduce(sends, keep, first, per, parts)
        gots = [lax.ppermute(send, "walker", other_core) for send in sends]
        shape = (keep.shape[1], keep.shape[2] // 2)
        sent = call(
            functools.partial(away_kernel, first, len(gots)), [(shape, BF)], info, keep, *gots
        )
        got_x = lax.ppermute(sent[0], "walker", [(v, v ^ 2) for v in range(4)])
        messages.append([keep, gots, [got_x], True, first, 1, parts])
        return sent

    def bring_home(message, n_parts, *earlier):
        keep, gots, others, turned, *_ = message
        if turned:
            homes = call(
                functools.partial(home_kernel, len(gots)),
                [((keep.shape[1] // n_parts, keep.shape[2] // 2), BF)] * n_parts,
                info, keep, *gots, after(others[0], *earlier),
            )
            others += [lax.ppermute(h, "walker", other_core) for h in homes]

    n = widths[0]
    parts = [(cw, (1, True, 0)), (cw, (0, True, 0)), (cw, (1, False, 0))]
    chunk_part = [(n, (0, False, 0))]

    def message_shapes(*sizes):
        return [((per, piece, size), BF) for size in sizes]

    e_keep, early, *sends = call(
        functools.partial(early_kernel, count, per, place),
        message_shapes(3 * cw) + [((samples, 2 * rw), BF)] + message_shapes(*[3 * cw // 4] * 4),
        info, o_rows, near, mid1, mid2, m0, m1, m2, m3, ow, far,
        cost=EARLY_COST,
    )
    reduce_rows(sends, e_keep, 0, parts)

    chunk, held_chunk = call(
        functools.partial(first_chunk_kernel, 0),
        [((samples, n), BF), ((rw, n), BF)],
        second, far, wide, far_grads[0],
        cost=FIRST_COST,
    )
    c_keep, send = call(
        functools.partial(early_chunk_kernel, per, place), message_shapes(n, n), info, early, chunk
    )
    reduce_rows([send], c_keep, 0, chunk_part)

    last2, held_chunk, chunk, messages[0][2], messages[1][2] = lax.optimization_barrier(
        (last2, held_chunk, chunk, messages[0][2], messages[1][2])
    )
    size = (3 * cw + n) // 2
    l_keep, last, *sends = call(
        functools.partial(late_kernel, count, per, late_slots),
        message_shapes(2 * size) + [((samples, rw), BF)] + message_shapes(*[cw, size - cw] * 2),
        info, last1, last2, m2, m3, ow, far, chunk, held, held_chunk,
        cost=LAST_COST,
    )
    sent = reduce_rows(sends, l_keep, per, parts + chunk_part)

    bring_home(messages[0], 1, *sent)
    bring_home(messages[1], 1, *sent)
    n = widths[1]
    (right,) = call(
        functools.partial(weigh_kernel, cuts[1]),
        [((samples, n), BF)],
        far, wide, far_grads[1],
        cost=WEIGH_COST,
    )
    messages[0][2], messages[1][2], right = lax.optimization_barrier(
        (messages[0][2], messages[1][2], right)
    )
    send, keep = call(
        functools.partial(chunk_kernel, per, place),
        [((2 * per, n, piece), BF)] * 2,
        info, early, second, last, after(right, *sent),
    )
    sent = reduce([send], keep, 0, 2 * per, [(None, (0, False, cuts[1]))])
    bring_home(messages[2], HOPS, *sent)

    flat, shapes = [], []
    for k, g, o, *what in messages:
        flat += [k, *g, *o]
        shapes.append((len(g), len(o), *what))
    return call(
        functools.partial(gather_kernel, count, shapes),
        [((piece, 2 * cw), F32)] * 2,
        info, *flat,
        scratch=[pltpu.VMEM((piece, 2 * cw), F32)] * 2 + [pltpu.SemaphoreType.DMA((HOPS, 2))],
        out_spec=pl.BlockSpec(memory_space=pl.ANY),
    )


def solution(mesh):
    in_specs = (
        P("walker", ("prow", "pcol")),
        P("walker", ("pcol", "prow")),
        P("walker", ("pcol", "prow")),
        P("walker"),
    )
    out_specs = (P(("prow", "walker"), "pcol"), P(("prow", "walker"), "pcol"))

    def per(*args):
        return tuple(per_device(*args))

    return jax.shard_map(
        per, mesh=mesh, in_specs=in_specs, out_specs=out_specs, check_vma=False
    )
```

```python
import functools

import jax
import jax.numpy as jnp
from jax import lax
from jax.experimental import pallas as pl
from jax.experimental.pallas import tpu as pltpu
from jax.sharding import PartitionSpec as P

BF = jnp.bfloat16
F32 = jnp.float32
VMEM = pl.BlockSpec(memory_space=pltpu.VMEM)
SMEM = pl.BlockSpec(memory_space=pltpu.SMEM)
MID, LOW, CORE, STRAIGHT, TABLE = 0, 1, 2, 3, 4
MEAN_COST, FAR_COST, EARLY_COST, FIRST_COST, LAST_COST = 6, 3, 6, 0, 2
WEIGH_COST, HOPS = 12, 4


def call(kernel, outs, *args, scratch=(), limit=24, cost=0, out_spec=VMEM):
    return pl.pallas_call(
        kernel,
        out_shape=[jax.ShapeDtypeStruct(s, d) for s, d in outs],
        in_specs=[SMEM if a.dtype == jnp.int32 else VMEM for a in args],
        out_specs=[out_spec] * len(outs),
        scratch_shapes=list(scratch),
        compiler_params=pltpu.CompilerParams(vmem_limit_bytes=limit * 2**20),
        cost_estimate=pl.CostEstimate(
            flops=int(cost * 1.15e9), bytes_accessed=0, transcendentals=0
        ),
    )(*args)


def after(value, *others):
    return lax.optimization_barrier((value,) + others)[0]


def centred(values, mean):
    return (values.astype(F32) - mean).astype(BF)


def weigh(energy, cols, grads):
    return (energy * cols.astype(F32) + grads.astype(F32)).astype(BF)


def dot(rows, right):
    return lax.dot_general(rows, right, (((0,), (0,)), ((), ())), preferred_element_type=F32)


def sums_kernel(rows, cols, out):
    width = rows.shape[1]
    out[:, :width] = jnp.sum(rows[...].astype(F32), axis=0, keepdims=True)
    out[:, width:] = jnp.sum(cols[...].astype(F32), axis=0, keepdims=True)


def own_kernel(count, cuts, cols, grads, energy, sums, out, wide, *pieces):
    width = cols.shape[1]
    lanes = wide.shape[1]
    d = centred(cols[...], sums[:, -width:] * (1 / count))
    out[:, :width] = d
    spread = jnp.broadcast_to(energy[...], wide.shape)
    wide[...] = spread
    for a in range(0, width, lanes):
        b = a + lanes
        out[:, width + a : width + b] = weigh(spread, d[:, a:b], grads[:, a:b])
    for a, b, piece in zip(cuts[:-1], cuts[1:], pieces):
        piece[...] = grads[:, a:b]


def by_core(info, walker, slot, sends, keep, value, turn=None):
    width = value.shape[-1]
    turn = width if turn is None else turn
    for core in (0, 1):

        @pl.when(info[CORE] == core)
        def _():
            for a, b, kept in ((0, turn, core == walker % 2), (turn, width, core != walker % 2)):
                if kept and a < b:
                    keep[slot, :, a:b] = value[:, a:b]
                start = 0
                for send in sends:
                    lo, hi = max(a, start), min(b, start + send.shape[-1])
                    if not kept and lo < hi:
                        send[slot, :, lo - start : hi - start] = value[:, lo:hi]
                    start += send.shape[-1]


def products(tile, rights):
    return jnp.concatenate([dot(tile, right[...]).astype(BF) for right in rights], axis=1)


def by_block(info, block, axis, per, slots, sends, keep, value):
    piece = value.shape[axis] // per
    turn = value.shape[1] // 2 if axis == 0 and per == 1 else None
    for i in range(per):
        at = slice(i * piece, (i + 1) * piece)
        walker = block * per + i
        part = value[at] if axis == 0 else value[:, at]
        by_core(info, walker, slots[walker], sends, keep, part, turn)


def low_or_high(info, then):
    for low in (1, 0):
        pl.when(info[LOW] == low)(functools.partial(then, 0 if low else 3, 3 if low else 0))


def mean_kernel(count, sums, m1, m2, out, near_mean, next_mean):
    rw = near_mean.shape[1]
    out[...] = sums[:, -out.shape[1] :] * (1 / count)
    near_mean[...] = m1[:, :rw] * (1 / count)
    next_mean[...] = m2[:, :rw] * (1 / count)


def far_kernel(raw, mean, out):
    out[...] = centred(raw[...], mean[...])


def early_kernel(
    count, per, slots,
    info, own_rows, near, mid1, mid2, m0, m1, m2, m3, ow, far,
    keep, early, *sends,
):
    rw = own_rows.shape[1]

    def group(there, beside):
        @pl.when(info[LOW] == 1)
        def _():
            early[:, rw:] = there
            early[:, :rw] = beside

        @pl.when(info[LOW] == 0)
        def _():
            early[:, :rw] = there
            early[:, rw:] = beside

    @pl.when(info[MID] == 1)
    def _():
        own = centred(own_rows[...], m0[:, :rw] * (1 / count))
        group(centred(mid1[...], m3[:, :rw] * (1 / count)), own)

    @pl.when(info[MID] == 0)
    def _():
        next_to = centred(near[...], m1[...])
        group(centred(mid2[...], m2[...]), next_to)

    result = products(early[...], (ow, far))
    for j, block in enumerate((1, 2)):
        by_block(info, block, 0, per, slots, sends, keep, result[j * rw : (j + 1) * rw])


def second_kernel(count, info, own_rows, near, m0, m1, ow, far, second, held):
    rw = own_rows.shape[1]

    @pl.when(info[MID] == 1)
    def _():
        second[...] = centred(near[...], m1[...])

    @pl.when(info[MID] == 0)
    def _():
        second[...] = centred(own_rows[...], m0[:, :rw] * (1 / count))

    held[...] = products(second[...], (ow, far))


def first_chunk_kernel(start, second, far, wide, grads, right, held):
    weigh_kernel(start, far, wide, grads, right)
    held[...] = products(second[...], (right,))


def early_chunk_kernel(per, slots, info, early, right, keep, send):
    rw = early.shape[1] // 2
    result = products(early[...], (right,))
    for j, block in enumerate((1, 2)):
        by_block(info, block, 0, per, slots, (send,), keep, result[j * rw : (j + 1) * rw])


def late_kernel(
    count, per, slots,
    info, last1, last2, m2, m3, ow, far, chunk, held, held_chunk,
    keep, tile, *sends,
):
    rw = last1.shape[1]

    @pl.when(info[MID] == 1)
    def _():
        tile[...] = centred(last1[...], m2[...])

    @pl.when(info[MID] == 0)
    def _():
        tile[...] = centred(last2[...], m3[:, :rw] * (1 / count))

    result = products(tile[...], (ow, far, chunk))
    before = jnp.concatenate((held[...], held_chunk[...]), axis=1)

    @functools.partial(low_or_high, info)
    def _(second_block, last_block):
        by_block(info, second_block, 0, per, slots, sends, keep, before)
        by_block(info, last_block, 0, per, slots, sends, keep, result)


def weigh_kernel(start, far, wide, grads, out):
    n, lanes = grads.shape[1], wide.shape[1]
    for a in range(0, n, lanes):
        cols = far[:, start + a : start + a + lanes]
        out[:, a : a + lanes] = weigh(wide[...], cols, grads[:, a : a + lanes])


def flipped_kernel(start, far, wide, grads, out):
    cols = far[:, start : start + grads.shape[1]]
    out[...] = weigh(wide[...], cols, grads[...]).T


def chunk_kernel(per, slots, kept, info, early, second, last, right, out):
    rw = last.shape[1]
    piece = rw // per

    def block_of(tile, first, block):
        for i in range(per):
            walker = block * per + i

            @pl.when((info[CORE] == walker % 2) == kept)
            def _():
                rows = tile[:, first + i * piece : first + (i + 1) * piece]
                out[slots[walker]] = lax.dot_general(
                    right[...], rows, (((1,), (0,)), ((), ())), preferred_element_type=F32
                ).astype(BF)

    block_of(early, 0, 1)
    block_of(early, rw, 2)

    @functools.partial(low_or_high, info)
    def _(second_block, last_block):
        block_of(second, 0, second_block)
        block_of(last, 0, last_block)


def pair(keep, gots, i):
    start, values = 0, []
    for got in gots:
        width = got.shape[2]
        values.append(keep[i, :, start : start + width].astype(F32) + got[i].astype(F32))
        start += width
    return jnp.concatenate(values, axis=1)


def pair_kernel(first, pieces, count, info, keep, *refs):
    gots, outs = refs[:count], refs[count:]
    for k, out in enumerate(outs, 1):
        i = jnp.clip(info[TABLE + k] - first, 0, pieces - 1)
        out[...] = pair(keep, gots, i).astype(BF)


def total(keep, gots, others, i):
    value = pair(keep, gots, i)
    for other in others:
        value = value + other[...].astype(F32)
    return value


def columns(keep, gots, lo, hi):
    start, values = 0, []
    for got in gots:
        a, b = max(lo, start), min(hi, start + got.shape[2])
        if a < b:
            values.append(keep[0, :, a:b].astype(F32) + got[0, :, a - start : b - start].astype(F32))
        start += got.shape[2]
    return jnp.concatenate(values, axis=1)


def away_kernel(first, count, info, keep, *refs):
    gots, out = refs[:count], refs[count]
    width = keep.shape[2]

    @pl.when(info[TABLE] == first)
    def _():
        out[...] = columns(keep, gots, width // 2, width).astype(BF)

    @pl.when(info[TABLE] != first)
    def _():
        out[...] = columns(keep, gots, 0, width // 2).astype(BF)


def home_kernel(count, info, keep, *refs):
    gots, got_x, outs = refs[:count], refs[count], refs[count + 1 :]
    width = keep.shape[2]
    value = (columns(keep, gots, width // 2, width) + got_x[...].astype(F32)).astype(BF)
    rows = value.shape[0] // len(outs)
    for i, out in enumerate(outs):
        out[...] = value[i * rows : (i + 1) * rows]


def gather_kernel(count, shapes, info, *refs):
    *refs, ham_out, corr_out, ham, corr, sems = refs
    rows, cw = ham.shape[0], ham.shape[1] // 2
    pos = info[TABLE]
    step = rows // HOPS

    def put(out, near, at, start, value):
        @pl.when((info[STRAIGHT] == 1) == near)
        def _():
            out[at, start : start + value.shape[1]] = value

        @pl.when((info[STRAIGHT] == 1) != near)
        def _():
            out[at, cw + start : cw + start + value.shape[1]] = value

    def spans(refs, start=0):
        for ref in refs:
            yield start, start + ref.shape[-1], ref
            start += ref.shape[-1]

    def place(parts, at, a, b, value):
        start = 0
        for size, (out, near, to) in parts:
            lo, hi = max(a, start), min(b, start + size)
            if lo < hi:
                some = value[:, lo - a : hi - a] * (1 / count)
                put((ham, corr)[out], near, at, to + lo - start, some)
            start += size

    def fill(k, keep, gots, others, turned, i, parts):
        at, width = slice(k * step, (k + 1) * step), keep.shape[2]
        for a, b, got in spans(gots):
            b = min(b, width // 2) if turned else b
            if a < b:
                value = keep[i, at, a:b].astype(F32) + got[i, at, : b - a].astype(F32)
                for other in others[:1] if turned else others:
                    value = value + other[at, a:b].astype(F32)
                place(parts, at, a, b, value)
        if turned:
            homes = others[1:]
            home = homes[k * len(homes) // HOPS]
            start = k * step % home.shape[0]
            place(parts, at, width // 2, width, home[start : start + step].astype(F32))

    def copies(k):
        at = slice(k * step, (k + 1) * step)
        return [
            pltpu.make_async_copy(ham.at[at], ham_out.at[at], sems.at[k, 0]),
            pltpu.make_async_copy(corr.at[at], corr_out.at[at], sems.at[k, 1]),
        ]

    start, messages = 0, []
    for n_gots, n_others, turned, first, pieces, parts in shapes:
        keep, gots = refs[start], refs[start + 1 : start + 1 + n_gots]
        others = refs[start + 1 + n_gots : start + 1 + n_gots + n_others]
        start += 1 + n_gots + n_others
        if parts[0][0] is None:
            out, near, to = parts[0][1]
            value = total(keep, gots, others, pos).T * (1 / count)
            put((ham, corr)[out], near, slice(None), to, value)
        else:
            messages.append((first, pieces, keep, gots, others, turned, parts))
    for k in range(HOPS):
        for first, pieces, keep, gots, others, turned, parts in messages:

            @pl.when((pos >= first) & (pos < first + pieces))
            def _():
                fill(k, keep, gots, others, turned, pos - first, parts)

        for copy in copies(k):
            copy.start()
    for k in range(HOPS):
        for copy in copies(k):
            copy.wait()


def per_device(o_rows, o_cols, grad_energy, energy):
    samples, rw = o_rows.shape
    cw = o_cols.shape[1]
    walkers = lax.axis_size("walker")
    chips = walkers // 2
    per = walkers // 4
    piece = rw // per
    w, y, z = (lax.axis_index(a) for a in ("walker", "prow", "pcol"))
    count = samples * walkers
    flip = [(0, 1), (1, 0)]
    outer = [(0, 1), (1, 0), (2, 3), (3, 2)]
    inner = [(1, 2), (2, 1)]
    ends = [(1, 0), (2, 3)]
    other_core = [(v, v ^ 1) for v in range(walkers)]

    order = [b * per + i for b in (1, 2, 0, 3) for i in range(per)]
    place = {v: [u for u in order if u % 2 == v % 2].index(v) for v in order}
    late_slots = {v: place[v] - per for v in order}
    table = [[place[(v + 2 * k) % walkers] for k in range(chips)] for v in range(walkers)]
    info = jnp.concatenate(
        (
            jnp.stack(((z == 1) | (z == 2), z < 2, w % 2, y == 0)).astype(jnp.int32),
            jnp.asarray(table, jnp.int32)[w],
        )
    )

    def shift(k, first, pieces):
        return [
            (v, (v + 2 * k) % walkers)
            for v in range(walkers)
            if first <= table[v][k] < first + pieces
        ]

    far_raw = lax.ppermute(o_cols, "prow", flip)
    near = lax.ppermute(o_rows, "pcol", outer)
    mid1 = lax.ppermute(o_rows, "pcol", inner)

    (sums,) = call(sums_kernel, [((1, rw + cw), F32)], o_rows, o_cols)
    m0 = lax.psum(sums, "walker")
    m1 = lax.ppermute(m0, "pcol", outer)
    m2 = lax.ppermute(m0, "pcol", [(0, 2), (1, 3), (2, 0), (3, 1)])

    column = energy[:, None]
    cuts = [0, cw // 2, cw]
    widths = [b - a for a, b in zip(cuts[:-1], cuts[1:])]
    ow, wide, *grads = call(
        functools.partial(own_kernel, count, cuts),
        [((samples, 2 * cw), BF), ((samples, min(widths)), F32)]
        + [((samples, n), BF) for n in widths],
        o_cols, grad_energy, column, m0,
    )

    near, mid1, m1, ow, m0, *grads = lax.optimization_barrier((near, mid1, m1, ow, m0, *grads))
    m3 = lax.ppermute(m0, "pcol", [(0, 3), (1, 2), (2, 1), (3, 0)])
    far_sums = lax.ppermute(m0, "prow", flip)
    mid2 = lax.ppermute(mid1, "pcol", ends)
    last1 = lax.ppermute(near, "pcol", inner)
    far_grads = [lax.ppermute(grads[0], "prow", flip)]

    far_mean, m1, m2 = call(
        functools.partial(mean_kernel, count),
        [((1, cw), F32), ((1, rw), F32), ((1, rw), F32)],
        far_sums, m1, m2,
        cost=MEAN_COST,
    )
    (far,) = call(far_kernel, [((samples, cw), BF)], far_raw, far_mean, cost=FAR_COST)
    second, held = call(
        functools.partial(second_kernel, count),
        [((samples, rw), BF), ((rw, 3 * cw), BF)],
        info, o_rows, near, m0, m1, ow, far,
    )
    last1, far, m3, second, held, *grads = lax.optimization_barrier(
        (last1, far, m3, second, held, *grads)
    )
    last2 = lax.ppermute(last1, "pcol", ends)
    far_grads += [lax.ppermute(g, "prow", flip) for g in grads[1:]]

    messages = []

    def reduce(sends, keep, first, pieces, parts):
        gots = [lax.ppermute(send, "walker", other_core) for send in sends]
        sent = call(
            functools.partial(pair_kernel, first, pieces, len(gots)),
            [(keep.shape[1:], BF)] * (chips - 1),
            info, keep, *gots,
        )
        others = [
            lax.ppermute(s, "walker", shift(k, first, pieces)) for k, s in enumerate(sent, 1)
        ]
        messages.append([keep, gots, others, False, first, pieces, parts])
        return sent

    def reduce_rows(sends, keep, first, parts):
        if per > 1:
            return reduce(sends, keep, first, per, parts)
        gots = [lax.ppermute(send, "walker", other_core) for send in sends]
        shape = (keep.shape[1], keep.shape[2] // 2)
        sent = call(
            functools.partial(away_kernel, first, len(gots)), [(shape, BF)], info, keep, *gots
        )
        got_x = lax.ppermute(sent[0], "walker", [(v, v ^ 2) for v in range(4)])
        messages.append([keep, gots, [got_x], True, first, 1, parts])
        return sent

    def bring_home(message, n_parts, *earlier):
        keep, gots, others, turned, *_ = message
        if turned:
            homes = call(
                functools.partial(home_kernel, len(gots)),
                [((keep.shape[1] // n_parts, keep.shape[2] // 2), BF)] * n_parts,
                info, keep, *gots, after(others[0], *earlier),
            )
            others += [lax.ppermute(h, "walker", other_core) for h in homes]

    n = widths[0]
    parts = [(cw, (1, True, 0)), (cw, (0, True, 0)), (cw, (1, False, 0))]
    chunk_part = [(n, (0, False, 0))]

    def message_shapes(*sizes):
        return [((per, piece, size), BF) for size in sizes]

    e_keep, early, *sends = call(
        functools.partial(early_kernel, count, per, place),
        message_shapes(3 * cw) + [((samples, 2 * rw), BF)] + message_shapes(*[3 * cw // 2] * 2),
        info, o_rows, near, mid1, mid2, m0, m1, m2, m3, ow, far,
        cost=EARLY_COST,
    )
    reduce_rows(sends, e_keep, 0, parts)

    chunk, held_chunk = call(
        functools.partial(first_chunk_kernel, 0),
        [((samples, n), BF), ((rw, n), BF)],
        second, far, wide, far_grads[0],
        cost=FIRST_COST,
    )
    c_keep, send = call(
        functools.partial(early_chunk_kernel, per, place), message_shapes(n, n), info, early, chunk
    )
    reduce_rows([send], c_keep, 0, chunk_part)

    last2, held_chunk, chunk, messages[0][2], messages[1][2] = lax.optimization_barrier(
        (last2, held_chunk, chunk, messages[0][2], messages[1][2])
    )
    size = (3 * cw + n) // 2
    l_keep, last, *sends = call(
        functools.partial(late_kernel, count, per, late_slots),
        message_shapes(2 * size) + [((samples, rw), BF)] + message_shapes(*[cw, size - cw] * 2),
        info, last1, last2, m2, m3, ow, far, chunk, held, held_chunk,
        cost=LAST_COST,
    )
    sent = reduce_rows(sends, l_keep, per, parts + chunk_part)

    bring_home(messages[0], 1, *sent)
    bring_home(messages[1], 1, *sent)
    n = widths[1]
    (right,) = call(
        functools.partial(flipped_kernel, cuts[1]),
        [((n, samples), BF)],
        far, wide, far_grads[1],
        cost=WEIGH_COST,
    )
    messages[0][2], messages[1][2], right = lax.optimization_barrier(
        (messages[0][2], messages[1][2], right)
    )
    right = after(right, *sent)
    send, keep = (
        call(
            functools.partial(chunk_kernel, per, place, kept),
            [((2 * per, n, piece), BF)],
            info, early, second, last, right,
        )[0]
        for kept in (False, True)
    )
    sent = reduce([send], keep, 0, 2 * per, [(None, (0, False, cuts[1]))])
    bring_home(messages[2], HOPS, *sent)

    flat, shapes = [], []
    for k, g, o, *what in messages:
        flat += [k, *g, *o]
        shapes.append((len(g), len(o), *what))
    return call(
        functools.partial(gather_kernel, count, shapes),
        [((piece, 2 * cw), F32)] * 2,
        info, *flat,
        scratch=[pltpu.VMEM((piece, 2 * cw), F32)] * 2 + [pltpu.SemaphoreType.DMA((HOPS, 2))],
        out_spec=pl.BlockSpec(memory_space=pl.ANY),
    )


def solution(mesh):
    in_specs = (
        P("walker", ("prow", "pcol")),
        P("walker", ("pcol", "prow")),
        P("walker", ("pcol", "prow")),
        P("walker"),
    )
    out_specs = (P(("prow", "walker"), "pcol"), P(("prow", "walker"), "pcol"))

    def per(*args):
        return tuple(per_device(*args))

    return jax.shard_map(
        per, mesh=mesh, in_specs=in_specs, out_specs=out_specs, check_vma=False
    )
```

```python
import functools

import jax
import jax.numpy as jnp
from jax import lax
from jax.experimental import pallas as pl
from jax.experimental.pallas import tpu as pltpu
from jax.sharding import PartitionSpec as P

BF = jnp.bfloat16
F32 = jnp.float32
VMEM = pl.BlockSpec(memory_space=pltpu.VMEM)
SMEM = pl.BlockSpec(memory_space=pltpu.SMEM)
MID, LOW, CORE, STRAIGHT, TABLE = 0, 1, 2, 3, 4
MEAN_COST, FAR_COST, EARLY_COST, FIRST_COST, LAST_COST = 6, 3, 4, 0, 0
WEIGH_COST, HOPS = 16, 4


def call(kernel, outs, *args, scratch=(), limit=24, cost=0, out_spec=VMEM):
    return pl.pallas_call(
        kernel,
        out_shape=[jax.ShapeDtypeStruct(s, d) for s, d in outs],
        in_specs=[SMEM if a.dtype == jnp.int32 else VMEM for a in args],
        out_specs=[out_spec] * len(outs),
        scratch_shapes=list(scratch),
        compiler_params=pltpu.CompilerParams(vmem_limit_bytes=limit * 2**20),
        cost_estimate=pl.CostEstimate(
            flops=int(cost * 1.15e9), bytes_accessed=0, transcendentals=0
        ),
    )(*args)


def after(value, *others):
    return lax.optimization_barrier((value,) + others)[0]


def centred(values, mean):
    return (values.astype(F32) - mean).astype(BF)


def weigh(energy, cols, grads):
    return (energy * cols.astype(F32) + grads.astype(F32)).astype(BF)


def dot(rows, right):
    return lax.dot_general(rows, right, (((0,), (0,)), ((), ())), preferred_element_type=F32)


def sums_kernel(rows, cols, out):
    width = rows.shape[1]
    out[:, :width] = jnp.sum(rows[...].astype(F32), axis=0, keepdims=True)
    out[:, width:] = jnp.sum(cols[...].astype(F32), axis=0, keepdims=True)


def own_kernel(count, cuts, cols, grads, energy, sums, out, wide, *pieces):
    width = cols.shape[1]
    lanes = wide.shape[1]
    d = centred(cols[...], sums[:, -width:] * (1 / count))
    out[:, :width] = d
    spread = jnp.broadcast_to(energy[...], wide.shape)
    wide[...] = spread
    for a in range(0, width, lanes):
        b = a + lanes
        out[:, width + a : width + b] = weigh(spread, d[:, a:b], grads[:, a:b])
    for a, b, piece in zip(cuts[:-1], cuts[1:], pieces):
        piece[...] = grads[:, a:b]


def by_core(info, walker, slot, sends, keep, value, turn=None):
    width = value.shape[-1]
    turn = width if turn is None else turn
    for core in (0, 1):

        @pl.when(info[CORE] == core)
        def _():
            for a, b, kept in ((0, turn, core == walker % 2), (turn, width, core != walker % 2)):
                if kept and a < b:
                    keep[slot, :, a:b] = value[:, a:b]
                start = 0
                for send in sends:
                    lo, hi = max(a, start), min(b, start + send.shape[-1])
                    if not kept and lo < hi:
                        send[slot, :, lo - start : hi - start] = value[:, lo:hi]
                    start += send.shape[-1]


def products(tile, rights):
    return jnp.concatenate([dot(tile, right[...]).astype(BF) for right in rights], axis=1)


def by_block(info, block, axis, per, slots, sends, keep, value):
    piece = value.shape[axis] // per
    turn = value.shape[1] // 2 if axis == 0 and per == 1 else None
    for i in range(per):
        at = slice(i * piece, (i + 1) * piece)
        walker = block * per + i
        part = value[at] if axis == 0 else value[:, at]
        by_core(info, walker, slots[walker], sends, keep, part, turn)


def low_or_high(info, then):
    for low in (1, 0):
        pl.when(info[LOW] == low)(functools.partial(then, 0 if low else 3, 3 if low else 0))


def mean_kernel(count, sums, m1, m2, out, near_mean, next_mean):
    rw = near_mean.shape[1]
    out[...] = sums[:, -out.shape[1] :] * (1 / count)
    near_mean[...] = m1[:, :rw] * (1 / count)
    next_mean[...] = m2[:, :rw] * (1 / count)


def far_kernel(raw, mean, out):
    out[...] = centred(raw[...], mean[...])


def early_kernel(
    count, per, slots,
    info, own_rows, near, mid1, mid2, m0, m1, m2, m3, ow, far,
    keep, early, *sends,
):
    rw = own_rows.shape[1]

    def group(there, beside):
        @pl.when(info[LOW] == 1)
        def _():
            early[:, rw:] = there
            early[:, :rw] = beside

        @pl.when(info[LOW] == 0)
        def _():
            early[:, :rw] = there
            early[:, rw:] = beside

    @pl.when(info[MID] == 1)
    def _():
        own = centred(own_rows[...], m0[:, :rw] * (1 / count))
        group(centred(mid1[...], m3[:, :rw] * (1 / count)), own)

    @pl.when(info[MID] == 0)
    def _():
        next_to = centred(near[...], m1[...])
        group(centred(mid2[...], m2[...]), next_to)

    result = products(early[...], (ow, far))
    for j, block in enumerate((1, 2)):
        by_block(info, block, 0, per, slots, sends, keep, result[j * rw : (j + 1) * rw])


def second_kernel(count, info, own_rows, near, m0, m1, ow, far, second, held):
    rw = own_rows.shape[1]

    @pl.when(info[MID] == 1)
    def _():
        second[...] = centred(near[...], m1[...])

    @pl.when(info[MID] == 0)
    def _():
        second[...] = centred(own_rows[...], m0[:, :rw] * (1 / count))

    held[...] = products(second[...], (ow, far))


def first_chunk_kernel(start, second, far, wide, grads, right, held):
    weigh_kernel(start, far, wide, grads, right)
    held[...] = products(second[...], (right,))


def early_chunk_kernel(per, slots, info, early, right, keep, send):
    rw = early.shape[1] // 2
    result = products(early[...], (right,))
    for j, block in enumerate((1, 2)):
        by_block(info, block, 0, per, slots, (send,), keep, result[j * rw : (j + 1) * rw])


def late_kernel(
    count, per, slots,
    info, last1, last2, m2, m3, ow, far, chunk, held, held_chunk,
    keep, tile, *sends,
):
    rw = last1.shape[1]

    @pl.when(info[MID] == 1)
    def _():
        tile[...] = centred(last1[...], m2[...])

    @pl.when(info[MID] == 0)
    def _():
        tile[...] = centred(last2[...], m3[:, :rw] * (1 / count))

    result = products(tile[...], (ow, far, chunk))
    before = jnp.concatenate((held[...], held_chunk[...]), axis=1)

    @functools.partial(low_or_high, info)
    def _(second_block, last_block):
        by_block(info, second_block, 0, per, slots, sends, keep, before)
        by_block(info, last_block, 0, per, slots, sends, keep, result)


def weigh_kernel(start, far, wide, grads, out):
    n, lanes = grads.shape[1], wide.shape[1]
    for a in range(0, n, lanes):
        cols = far[:, start + a : start + a + lanes]
        out[:, a : a + lanes] = weigh(wide[...], cols, grads[:, a : a + lanes])


def chunk_kernel(per, slots, info, early, second, last, right_ref, send, keep):
    rw = last.shape[1]
    right = right_ref[...]
    result = dot(right, early[...]).astype(BF)
    for j, block in enumerate((1, 2)):
        by_block(info, block, 1, per, slots, (send,), keep, result[:, j * rw : (j + 1) * rw])
    of_second = dot(right, second[...]).astype(BF)
    of_last = dot(right, last[...]).astype(BF)

    @functools.partial(low_or_high, info)
    def _(second_block, last_block):
        by_block(info, second_block, 1, per, slots, (send,), keep, of_second)
        by_block(info, last_block, 1, per, slots, (send,), keep, of_last)


def pair(keep, gots, i):
    start, values = 0, []
    for got in gots:
        width = got.shape[2]
        values.append(keep[i, :, start : start + width].astype(F32) + got[i].astype(F32))
        start += width
    return jnp.concatenate(values, axis=1)


def pair_kernel(first, pieces, count, info, keep, *refs):
    gots, outs = refs[:count], refs[count:]
    for k, out in enumerate(outs, 1):
        i = jnp.clip(info[TABLE + k] - first, 0, pieces - 1)
        out[...] = pair(keep, gots, i).astype(BF)


def total(keep, gots, others, i):
    value = pair(keep, gots, i)
    for other in others:
        value = value + other[...].astype(F32)
    return value


def columns(keep, gots, lo, hi):
    start, values = 0, []
    for got in gots:
        a, b = max(lo, start), min(hi, start + got.shape[2])
        if a < b:
            values.append(keep[0, :, a:b].astype(F32) + got[0, :, a - start : b - start].astype(F32))
        start += got.shape[2]
    return jnp.concatenate(values, axis=1)


def away_kernel(first, count, info, keep, *refs):
    gots, out = refs[:count], refs[count]
    width = keep.shape[2]

    @pl.when(info[TABLE] == first)
    def _():
        out[...] = columns(keep, gots, width // 2, width).astype(BF)

    @pl.when(info[TABLE] != first)
    def _():
        out[...] = columns(keep, gots, 0, width // 2).astype(BF)


def home_kernel(count, info, keep, *refs):
    gots, got_x, outs = refs[:count], refs[count], refs[count + 1 :]
    width = keep.shape[2]
    value = (columns(keep, gots, width // 2, width) + got_x[...].astype(F32)).astype(BF)
    rows = value.shape[0] // len(outs)
    for i, out in enumerate(outs):
        out[...] = value[i * rows : (i + 1) * rows]


def gather_kernel(count, shapes, info, *refs):
    *refs, ham_out, corr_out, ham, corr, sems = refs
    rows, cw = ham.shape[0], ham.shape[1] // 2
    pos = info[TABLE]
    step = rows // HOPS

    def put(out, near, at, start, value):
        @pl.when((info[STRAIGHT] == 1) == near)
        def _():
            out[at, start : start + value.shape[1]] = value

        @pl.when((info[STRAIGHT] == 1) != near)
        def _():
            out[at, cw + start : cw + start + value.shape[1]] = value

    def spans(refs, start=0):
        for ref in refs:
            yield start, start + ref.shape[-1], ref
            start += ref.shape[-1]

    def place(parts, at, a, b, value):
        start = 0
        for size, (out, near, to) in parts:
            lo, hi = max(a, start), min(b, start + size)
            if lo < hi:
                some = value[:, lo - a : hi - a] * (1 / count)
                put((ham, corr)[out], near, at, to + lo - start, some)
            start += size

    def fill(k, keep, gots, others, turned, i, parts):
        at, width = slice(k * step, (k + 1) * step), keep.shape[2]
        for a, b, got in spans(gots):
            b = min(b, width // 2) if turned else b
            if a < b:
                value = keep[i, at, a:b].astype(F32) + got[i, at, : b - a].astype(F32)
                for other in others[:1] if turned else others:
                    value = value + other[at, a:b].astype(F32)
                place(parts, at, a, b, value)
        if turned:
            homes = others[1:]
            home = homes[k * len(homes) // HOPS]
            start = k * step % home.shape[0]
            place(parts, at, width // 2, width, home[start : start + step].astype(F32))

    def copies(k):
        at = slice(k * step, (k + 1) * step)
        return [
            pltpu.make_async_copy(ham.at[at], ham_out.at[at], sems.at[k, 0]),
            pltpu.make_async_copy(corr.at[at], corr_out.at[at], sems.at[k, 1]),
        ]

    start, messages = 0, []
    for n_gots, n_others, turned, first, pieces, parts in shapes:
        keep, gots = refs[start], refs[start + 1 : start + 1 + n_gots]
        others = refs[start + 1 + n_gots : start + 1 + n_gots + n_others]
        start += 1 + n_gots + n_others
        if parts[0][0] is None:
            out, near, to = parts[0][1]
            value = total(keep, gots, others, pos).T * (1 / count)
            put((ham, corr)[out], near, slice(None), to, value)
        else:
            messages.append((first, pieces, keep, gots, others, turned, parts))
    for k in range(HOPS):
        for first, pieces, keep, gots, others, turned, parts in messages:

            @pl.when((pos >= first) & (pos < first + pieces))
            def _():
                fill(k, keep, gots, others, turned, pos - first, parts)

        for copy in copies(k):
            copy.start()
    for k in range(HOPS):
        for copy in copies(k):
            copy.wait()


def per_device(o_rows, o_cols, grad_energy, energy):
    samples, rw = o_rows.shape
    cw = o_cols.shape[1]
    walkers = lax.axis_size("walker")
    chips = walkers // 2
    per = walkers // 4
    piece = rw // per
    w, y, z = (lax.axis_index(a) for a in ("walker", "prow", "pcol"))
    count = samples * walkers
    flip = [(0, 1), (1, 0)]
    outer = [(0, 1), (1, 0), (2, 3), (3, 2)]
    inner = [(1, 2), (2, 1)]
    ends = [(1, 0), (2, 3)]
    other_core = [(v, v ^ 1) for v in range(walkers)]

    order = [b * per + i for b in (1, 2, 0, 3) for i in range(per)]
    place = {v: [u for u in order if u % 2 == v % 2].index(v) for v in order}
    late_slots = {v: place[v] - per for v in order}
    table = [[place[(v + 2 * k) % walkers] for k in range(chips)] for v in range(walkers)]
    info = jnp.concatenate(
        (
            jnp.stack(((z == 1) | (z == 2), z < 2, w % 2, y == 0)).astype(jnp.int32),
            jnp.asarray(table, jnp.int32)[w],
        )
    )

    def shift(k, first, pieces):
        return [
            (v, (v + 2 * k) % walkers)
            for v in range(walkers)
            if first <= table[v][k] < first + pieces
        ]

    far_raw = lax.ppermute(o_cols, "prow", flip)
    mid1 = lax.ppermute(o_rows, "pcol", inner)
    near = lax.ppermute(o_rows, "pcol", outer)

    (sums,) = call(sums_kernel, [((1, rw + cw), F32)], o_rows, o_cols)
    m0 = lax.psum(sums, "walker")
    m1 = lax.ppermute(m0, "pcol", outer)
    m2 = lax.ppermute(m0, "pcol", [(0, 2), (1, 3), (2, 0), (3, 1)])

    column = energy[:, None]
    cuts = [0, cw // 2, cw]
    widths = [b - a for a, b in zip(cuts[:-1], cuts[1:])]
    ow, wide, *grads = call(
        functools.partial(own_kernel, count, cuts),
        [((samples, 2 * cw), BF), ((samples, min(widths)), F32)]
        + [((samples, n), BF) for n in widths],
        o_cols, grad_energy, column, m0,
    )

    near, mid1, m1, ow, m0, *grads = lax.optimization_barrier((near, mid1, m1, ow, m0, *grads))
    m3 = lax.ppermute(m0, "pcol", [(0, 3), (1, 2), (2, 1), (3, 0)])
    far_sums = lax.ppermute(m0, "prow", flip)
    mid2 = lax.ppermute(mid1, "pcol", ends)
    last1 = lax.ppermute(near, "pcol", inner)
    far_grads = [lax.ppermute(grads[0], "prow", flip)]

    far_mean, m1, m2 = call(
        functools.partial(mean_kernel, count),
        [((1, cw), F32), ((1, rw), F32), ((1, rw), F32)],
        far_sums, m1, m2,
        cost=MEAN_COST,
    )
    (far,) = call(far_kernel, [((samples, cw), BF)], far_raw, far_mean, cost=FAR_COST)
    second, held = call(
        functools.partial(second_kernel, count),
        [((samples, rw), BF), ((rw, 3 * cw), BF)],
        info, o_rows, near, m0, m1, ow, far,
    )
    last1, far, m3, second, held, *grads = lax.optimization_barrier(
        (last1, far, m3, second, held, *grads)
    )
    last2 = lax.ppermute(last1, "pcol", ends)
    far_grads += [lax.ppermute(g, "prow", flip) for g in grads[1:]]

    messages = []

    def reduce(sends, keep, first, pieces, parts):
        gots = [lax.ppermute(send, "walker", other_core) for send in sends]
        sent = call(
            functools.partial(pair_kernel, first, pieces, len(gots)),
            [(keep.shape[1:], BF)] * (chips - 1),
            info, keep, *gots,
        )
        others = [
            lax.ppermute(s, "walker", shift(k, first, pieces)) for k, s in enumerate(sent, 1)
        ]
        messages.append([keep, gots, others, False, first, pieces, parts])
        return sent

    def reduce_rows(sends, keep, first, parts):
        if per > 1:
            return reduce(sends, keep, first, per, parts)
        gots = [lax.ppermute(send, "walker", other_core) for send in sends]
        shape = (keep.shape[1], keep.shape[2] // 2)
        sent = call(
            functools.partial(away_kernel, first, len(gots)), [(shape, BF)], info, keep, *gots
        )
        got_x = lax.ppermute(sent[0], "walker", [(v, v ^ 2) for v in range(4)])
        messages.append([keep, gots, [got_x], True, first, 1, parts])
        return sent

    def bring_home(message, n_parts, *earlier):
        keep, gots, others, turned, *_ = message
        if turned:
            homes = call(
                functools.partial(home_kernel, len(gots)),
                [((keep.shape[1] // n_parts, keep.shape[2] // 2), BF)] * n_parts,
                info, keep, *gots, after(others[0], *earlier),
            )
            others += [lax.ppermute(h, "walker", other_core) for h in homes]

    n = widths[0]
    parts = [(cw, (1, True, 0)), (cw, (0, True, 0)), (cw, (1, False, 0))]
    chunk_part = [(n, (0, False, 0))]

    def message_shapes(*sizes):
        return [((per, piece, size), BF) for size in sizes]

    e_keep, early, *sends = call(
        functools.partial(early_kernel, count, per, place),
        message_shapes(3 * cw) + [((samples, 2 * rw), BF)] + message_shapes(*[3 * cw // 2] * 2),
        info, o_rows, near, mid1, mid2, m0, m1, m2, m3, ow, far,
        cost=EARLY_COST,
    )
    reduce_rows(sends, e_keep, 0, parts)

    chunk, held_chunk = call(
        functools.partial(first_chunk_kernel, 0),
        [((samples, n), BF), ((rw, n), BF)],
        second, far, wide, far_grads[0],
        cost=FIRST_COST,
    )
    c_keep, send = call(
        functools.partial(early_chunk_kernel, per, place), message_shapes(n, n), info, early, chunk
    )
    reduce_rows([send], c_keep, 0, chunk_part)

    last2, held_chunk, chunk, messages[0][2], messages[1][2] = lax.optimization_barrier(
        (last2, held_chunk, chunk, messages[0][2], messages[1][2])
    )
    size = (3 * cw + n) // 2
    l_keep, last, *sends = call(
        functools.partial(late_kernel, count, per, late_slots),
        message_shapes(2 * size) + [((samples, rw), BF)] + message_shapes(*[cw, size - cw] * 2),
        info, last1, last2, m2, m3, ow, far, chunk, held, held_chunk,
        cost=LAST_COST,
    )
    sent = reduce_rows(sends, l_keep, per, parts + chunk_part)

    bring_home(messages[0], 1, *sent)
    bring_home(messages[1], 1, *sent)
    n = widths[1]
    (right,) = call(
        functools.partial(weigh_kernel, cuts[1]),
        [((samples, n), BF)],
        far, wide, far_grads[1],
        cost=WEIGH_COST,
    )
    messages[0][2], messages[1][2], right = lax.optimization_barrier(
        (messages[0][2], messages[1][2], right)
    )
    send, keep = call(
        functools.partial(chunk_kernel, per, place),
        [((2 * per, n, piece), BF)] * 2,
        info, early, second, last, after(right, *sent),
    )
    sent = reduce([send], keep, 0, 2 * per, [(None, (0, False, cuts[1]))])
    bring_home(messages[2], HOPS, *sent)

    flat, shapes = [], []
    for k, g, o, *what in messages:
        flat += [k, *g, *o]
        shapes.append((len(g), len(o), *what))
    return call(
        functools.partial(gather_kernel, count, shapes),
        [((piece, 2 * cw), F32)] * 2,
        info, *flat,
        scratch=[pltpu.VMEM((piece, 2 * cw), F32)] * 2 + [pltpu.SemaphoreType.DMA((HOPS, 2))],
        out_spec=pl.BlockSpec(memory_space=pl.ANY),
    )


def solution(mesh):
    in_specs = (
        P("walker", ("prow", "pcol")),
        P("walker", ("pcol", "prow")),
        P("walker", ("pcol", "prow")),
        P("walker"),
    )
    out_specs = (P(("prow", "walker"), "pcol"), P(("prow", "walker"), "pcol"))

    def per(*args):
        return tuple(per_device(*args))

    return jax.shard_map(
        per, mesh=mesh, in_specs=in_specs, out_specs=out_specs, check_vma=False
    )
```
